128 devices in a mesh: section: 8 (over y, x_lo), seq: 16 (over z, x_hi, core).
Axes of the slice: x: 4 (x_hi: 2, x_lo: 2; x = x_hi * 2 + x_lo), y: 4, z: 4, core: 2. Of those that a mesh axis runs over, the one named last changes fastest.
Arguments:
- activations: bfloat16 [8, 2048, 3584], P('section', 'seq'), may hold values from -80 to 80
- incoming: bfloat16 [2048, 3584], P('seq'), may hold values from -4 to 4
- column_ids: int32 [9, 2048], replicated, may hold values from 0 to 11, as said below
- positions: int32 [9, 2048], replicated, may hold values from 0 to 23, as said below
- norm_gain: float32 [8, 3584], P('section')
- w_query: bfloat16 [8, 3584, 1792], P('section', 'seq')
- w_key: bfloat16 [8, 3584, 256], P('section', 'seq')
- w_value: bfloat16 [8, 3584, 256], P('section', 'seq'), may hold values from -0.09375 to 0.09375
- w_out: bfloat16 [8, 1792, 3584], P('section', 'seq'), may hold values from -0.125 to 0.125
- b_query: float32 [8, 1792], P('section'), may hold values from -4 to 4
- b_key: float32 [8, 256], P('section'), may hold values from -4 to 4
- b_value: float32 [8, 256], P('section'), may hold values from -3 to 3
Outputs:
- first_pass: bfloat16 [8, 2048, 3584], P('section', 'seq')
- second_pass: bfloat16 [8, 2048, 3584], P('section', 'seq')
The draws below stay inside these ranges and needn't reach their ends.
Inputs may be any that keep to these rules, and one draw needn't show every extreme that they name: `column_ids`: each row is one serialized table: runs of one or two consecutive tokens form cells, the cells take the column numbers 0, 1, ..., 11 in turn, table row after table row; column 0 is a row's header cell. The first table row of every micro-batch has two tokens in each cell. `positions`: A token's position counts the tokens since its table row began.
All inputs are finite; a program needn't handle non-finite values.
Results may differ from the reference program's by a relative error of at most 0.012.
Values may be sent and summed in bfloat16 or wider, within the bound.
No kernel may reach another device: no remote copies, remote signals or barrier semaphores. Data moves between devices by JAX's collectives and lax.ppermute only.
A program may use at most 128 MiB of HBM per device.

```python
import math
import jax
import jax.numpy as jnp
from jax import lax

D = 3584
HEAD_DIM = 128
HEADS = 14
KV_HEADS = 2
NCOL = 12
QW = 1792
KVW = 256
SEQ = 2048
SECTIONS = 8
MICRO = 9
N_SECTION = 8


def table_layout(key):
    index = jnp.broadcast_to(jnp.arange(SEQ, dtype=jnp.int32)[None, :], (MICRO, SEQ))
    random_starts = jax.random.randint(key, (MICRO, SEQ), 0, 2) == 0
    random_starts = random_starts | (index == 2 * NCOL)
    previous = jnp.concatenate([jnp.ones((MICRO, 1), jnp.bool_), random_starts[:, :-1]], axis=1)
    random_starts = random_starts | jnp.logical_not(previous)
    leading = index < 2 * NCOL
    starts = jnp.where(leading, index % 2 == 0, random_starts)
    starts = starts | (index == 0) | (index == 2 * NCOL)
    cells = jnp.cumsum(starts.astype(jnp.int32), axis=1) - 1
    columns = cells % NCOL
    row_start = starts & (columns == 0)
    begins = lax.cummax(jnp.where(row_start, index, 0), axis=1)
    return (columns.astype(jnp.int32), (index - begins).astype(jnp.int32))


def draw_column_ids(key, part):
    columns, places = table_layout(jax.random.fold_in(key, 31))
    return columns


def draw_positions(key, part):
    columns, places = table_layout(jax.random.fold_in(key, 31))
    return places


def draw_activations(key, part):
    shape = (SECTIONS, SEQ, D)
    base = jax.random.truncated_normal(jax.random.fold_in(key, 3), -4.0, 4.0, shape, jnp.float32)
    return base.astype(jnp.bfloat16)


def draw_norm_gain(key, part):
    shape = (SECTIONS, D)
    return jnp.exp(jax.random.uniform(key, shape, jnp.float32, math.log(0.5), math.log(2.0)))


def query_base(key):
    return jax.random.truncated_normal(jax.random.fold_in(key, 101), -4.0, 4.0, (SECTIONS, D, HEADS * HEAD_DIM), jnp.float32) * D ** (-0.5)


def draw_w_query(key, part):
    return query_base(key).astype(jnp.bfloat16)


def draw_w_key(key, part):
    noise = jax.random.truncated_normal(jax.random.fold_in(key, 202), -4.0, 4.0, (SECTIONS, D, KV_HEADS * HEAD_DIM), jnp.float32) * D ** (-0.5)
    return noise.astype(jnp.bfloat16)


def block_scale(stream_key, shape, pieces, least, top_value):
    def one(axis_at, blocks):
        steps = jax.random.uniform(jax.random.fold_in(jax.random.fold_in(stream_key, 6), axis_at), (blocks,), jnp.float32, least / len(pieces), top_value / len(pieces))
        return jnp.repeat(jnp.exp(steps), shape[axis_at] // blocks).reshape((-1,) + (1,) * (len(shape) - axis_at - 1))

    level = one(*pieces[0])
    for cut in pieces[1:]:
        level = level * one(*cut)
    return level


def centred(key, shape, scale, reach, shards=(), kind=jnp.bfloat16):
    values = jax.random.normal(key, shape, jnp.float32) * scale
    if len(shards) > 0:
        values = block_scale(key, shape, shards, -0.22, 0.18) * values
    return jnp.clip(values, min=-reach, max=reach).astype(kind)


def setup_inputs(seed: int = 0) -> dict:
    key_of = jax.random.split(jax.random.key(seed), 13)
    return {
        "activations": draw_activations(jax.random.fold_in(key_of[12], 71), 0),
        "incoming": centred(key_of[1], (SEQ, D), 1.0, 4.0, ((0, 16),)),
        "column_ids": draw_column_ids(jax.random.fold_in(key_of[12], 71), 0),
        "positions": draw_positions(jax.random.fold_in(key_of[12], 71), 0),
        "norm_gain": draw_norm_gain(jax.random.fold_in(key_of[12], 71), 0),
        "w_query": draw_w_query(jax.random.fold_in(key_of[12], 71), 0),
        "w_key": draw_w_key(jax.random.fold_in(key_of[12], 71), 0),
        "w_value": centred(key_of[7], (SECTIONS, D, KVW), D ** -0.5, 0.09375, ((0, 8), (1, 16))),
        "w_out": centred(key_of[8], (SECTIONS, QW, D), QW ** -0.5, 0.125, ((0, 8), (1, 16))),
        "b_query": centred(key_of[9], (SECTIONS, QW), 1.0, 4.0, ((0, 8),), jnp.float32),
        "b_key": centred(key_of[10], (SECTIONS, KVW), 1.0, 4.0, ((0, 8),), jnp.float32),
        "b_value": centred(key_of[11], (SECTIONS, KVW), 0.5, 3.0, ((0, 8),), jnp.float32),
    }


EPSILON = 1e-06
THETA = 1000000.0

def rotate(entries, places):
    half = entries.shape[-1] // 2
    freqs = THETA ** (-(jnp.arange(half, dtype=jnp.float32) * 2.0) / entries.shape[-1])
    angles = places.astype(jnp.float32)[:, None] * freqs[None, :]
    cosine = jnp.cos(angles)[:, None, :]
    sine = jnp.sin(angles)[:, None, :]
    first = entries[..., :half]
    second = entries[..., half:]
    return jnp.concatenate([first * cosine - second * sine, second * cosine + first * sine], axis=-1)

def section_layer(inputs, gain, query_weight, key_weight, value_weight, out_weight, query_bias, key_bias, value_bias, columns, places):
    length = inputs.shape[0]
    wide = inputs.astype(jnp.float32)
    hidden = (wide * lax.rsqrt(lax.optimization_barrier(jnp.mean(wide * wide, axis=-1, keepdims=True)) + EPSILON) * gain).astype(jnp.bfloat16)
    queries = rotate((jnp.dot(hidden, query_weight, preferred_element_type=jnp.float32) + query_bias).reshape(length, HEADS, HEAD_DIM), places).astype(jnp.bfloat16)
    keys_rot = rotate((jnp.dot(hidden, key_weight, preferred_element_type=jnp.float32) + key_bias).reshape(length, KV_HEADS, HEAD_DIM), places).astype(jnp.bfloat16)
    values = (jnp.dot(hidden, value_weight, preferred_element_type=jnp.float32) + value_bias).astype(jnp.bfloat16).reshape(length, KV_HEADS, HEAD_DIM)
    index = jnp.arange(length, dtype=jnp.int32)
    allowed = (index[None, :] <= index[:, None]) & ((columns[None, :] == columns[:, None]) | (columns[None, :] == 0))
    group = HEADS // KV_HEADS
    scale = HEAD_DIM ** (-0.5)
    head_queries = jnp.transpose(queries, (1, 0, 2))
    head_keys = jnp.repeat(jnp.transpose(keys_rot, (1, 0, 2)), group, axis=0)
    head_values = jnp.repeat(jnp.transpose(values, (1, 0, 2)), group, axis=0)

    def one_head(operands):
        query_head, key_head, value_head = operands
        scores = jnp.dot(query_head, key_head.T, preferred_element_type=jnp.float32) * scale
        scores = jnp.where(allowed, scores, -1e+30)
        top = lax.optimization_barrier(jnp.max(scores, axis=-1, keepdims=True))
        exponentials = jnp.where(allowed, jnp.exp(scores - top), 0.0)
        probs = exponentials.astype(jnp.bfloat16)
        summed = jnp.dot(probs, value_head, preferred_element_type=jnp.float32)
        return summed / lax.optimization_barrier(jnp.sum(exponentials, axis=-1, keepdims=True))
    mixed = lax.map(one_head, (head_queries, head_keys, head_values))
    context = jnp.transpose(mixed, (1, 0, 2)).reshape(length, HEADS * HEAD_DIM).astype(jnp.bfloat16)
    return (wide + jnp.dot(context, out_weight, preferred_element_type=jnp.float32)).astype(jnp.bfloat16)

def apply_section(inputs, layer_index, micro_row, norm_gain, w_query, w_key, w_value, w_out, b_query, b_key, b_value, column_ids, positions):
    return section_layer(inputs, norm_gain[layer_index], w_query[layer_index], w_key[layer_index], w_value[layer_index], w_out[layer_index], b_query[layer_index], b_key[layer_index], b_value[layer_index], column_ids[micro_row], positions[micro_row])

def reference(activations, incoming, column_ids, positions, norm_gain, w_query, w_key, w_value, w_out, b_query, b_key, b_value):
    firsts = []
    for layer_index in range(N_SECTION):
        firsts.append(apply_section(activations[layer_index], layer_index, layer_index, norm_gain, w_query, w_key, w_value, w_out, b_query, b_key, b_value, column_ids, positions))
    seconds = []
    for layer_index in range(N_SECTION):
        if layer_index == 0:
            source = incoming
            micro_row = N_SECTION
        else:
            source = firsts[layer_index - 1]
            micro_row = layer_index - 1
        seconds.append(apply_section(source, layer_index, micro_row, norm_gain, w_query, w_key, w_value, w_out, b_query, b_key, b_value, column_ids, positions))
    return (jnp.stack(firsts), jnp.stack(seconds))
```

```python
import functools

import jax
import jax.numpy as jnp
from jax import lax
from jax.experimental import pallas as pl
from jax.experimental.pallas import tpu as pltpu
from jax.sharding import PartitionSpec as P

HEAD_DIM = 128
HEADS = 14
KV_HEADS = 2
GROUP = HEADS // KV_HEADS
D = 3584
HALF = D // 2
QH = GROUP * HEAD_DIM
CAT = QH + 2 * HEAD_DIM
EPSILON = 1e-06
THETA = 1000000.0
NZ, NX, NC = 4, 2, 2
CHIPS = NZ * NX
SCORE = HEAD_DIM ** (-0.5) * 1.4426950408889634
VMEM = pltpu.MemorySpace.VMEM
SMEM = pltpu.MemorySpace.SMEM


def shift(move):
    pairs = []
    for z in range(NZ):
        for x in range(NX):
            for c in range(NC):
                a, b, d = move(z, x, c)
                pairs.append(((z * NX + x) * NC + c, ((a % NZ) * NX + b) * NC + d))
    return pairs


UP = shift(lambda z, x, c: (z + 1, x, c))
DOWN = shift(lambda z, x, c: (z - 1, x, c))
ACROSS = shift(lambda z, x, c: (z, 1 - x, c))
CORE = shift(lambda z, x, c: (z, x, 1 - c))


def send(value, pairs):
    return lax.ppermute(value, "seq", pairs)


def spread(first, second):
    up_a, down_a, across_a = send(first, UP), send(first, DOWN), send(first, ACROSS)
    up_b, down_b, across_b = send(second, UP), send(second, DOWN), send(second, ACROSS)
    far_a = send(up_a, UP)
    far_b = send(down_b, DOWN)
    cross_up_a, cross_down_a = send(across_a, UP), send(across_a, DOWN)
    cross_up_b, cross_down_b = send(across_b, UP), send(across_b, DOWN)
    cross_far_a, cross_far_b = send(far_a, ACROSS), send(far_b, ACROSS)
    return [
        first, up_a, down_a, across_a, far_a, cross_up_a, cross_down_a, cross_far_a,
        second, up_b, down_b, across_b, far_b, cross_up_b, cross_down_b, cross_far_b,
    ]


def piece_ids(z, x, first_half, second_half):
    chips = [
        z * NX + x,
        (z + 3) % NZ * NX + x,
        (z + 1) % NZ * NX + x,
        z * NX + 1 - x,
        (z + 2) % NZ * NX + x,
        (z + 3) % NZ * NX + 1 - x,
        (z + 1) % NZ * NX + 1 - x,
        (z + 2) % NZ * NX + 1 - x,
    ]
    return jnp.stack(
        [k * 2 + first_half for k in chips] + [k * 2 + second_half for k in chips]
    ).astype(jnp.int32)


def start_copies(ids, pieces, whole, sems):
    rows = pieces[0].shape[0]
    copies = []
    for n, piece in enumerate(pieces):
        at = pl.multiple_of(ids[n] * rows, 16)
        copy = pltpu.make_async_copy(piece, whole.at[pl.ds(at, rows)], sems.at[n])
        copy.start()
        copies.append(copy)
    return copies


def project_kernel(ids, own, other, gain, bias, cosine, sine, *rest):
    pieces, (q_out, kv_out), (whole, hidden, sems) = rest[:16], rest[16:18], rest[18:]
    copies = start_copies(ids, pieces, whole, sems)
    core = ids[16]
    at_own = pl.multiple_of(core * HALF, 128)
    at_other = pl.multiple_of((1 - core) * HALF, 128)
    rows = 64

    def norm(n, _):
        r = pl.ds(pl.multiple_of(n * rows, rows), rows)
        a = own[r, :].astype(jnp.float32)
        b = other[r, :].astype(jnp.float32)
        total = jnp.sum(a * a, axis=-1, keepdims=True) + jnp.sum(b * b, axis=-1, keepdims=True)
        inverse = lax.rsqrt(total * (1.0 / D) + EPSILON)
        hidden[r, pl.ds(at_own, HALF)] = (a * inverse * gain[:, pl.ds(at_own, HALF)]).astype(jnp.bfloat16)
        hidden[r, pl.ds(at_other, HALF)] = (b * inverse * gain[:, pl.ds(at_other, HALF)]).astype(jnp.bfloat16)
        return 0

    lax.fori_loop(0, own.shape[0] // rows, norm, 0)
    for copy in copies:
        copy.wait()
    for n in range(0, CAT, 128):
        y = jnp.dot(hidden[...], whole[:, n : n + 128], preferred_element_type=jnp.float32)
        y = y + bias[:, n : n + 128]
        if n < QH + HEAD_DIM:
            y = y * cosine[...] + pltpu.roll(y, HEAD_DIM // 2, 1) * sine[...]
        if n < QH:
            q_out[n // HEAD_DIM] = y.astype(jnp.bfloat16)
        else:
            kv_out[:, n - QH : n - QH + 128] = y.astype(jnp.bfloat16)


def project(ids, own, other, gain, bias, cosine, sine, pieces):
    tokens = own.shape[0]
    any_space = pl.BlockSpec(memory_space=pl.ANY)
    vmem = pl.BlockSpec(memory_space=VMEM)
    return pl.pallas_call(
        project_kernel,
        out_shape=(
            jax.ShapeDtypeStruct((GROUP, tokens, HEAD_DIM), jnp.bfloat16),
            jax.ShapeDtypeStruct((tokens, 2 * HEAD_DIM), jnp.bfloat16),
        ),
        in_specs=[pl.BlockSpec(memory_space=SMEM)] + [vmem] * 6 + [any_space] * 16,
        out_specs=(vmem, vmem),
        scratch_shapes=[
            pltpu.VMEM((D, CAT), jnp.bfloat16),
            pltpu.VMEM((tokens, D), jnp.bfloat16),
            pltpu.SemaphoreType.DMA((16,)),
        ],
        compiler_params=pltpu.CompilerParams(vmem_limit_bytes=24 * 1024 * 1024),
        cost_estimate=pl.CostEstimate(
            flops=2 * tokens * D * CAT, bytes_accessed=2 * D * CAT, transcendentals=0
        ),
    )(ids, own, other, gain, bias, cosine, sine, *pieces)


def attend_kernel(ids, queries, mask, *rest):
    pieces, context, (whole, sems) = rest[:16], rest[16], rest[17:]
    copies = start_copies(ids, pieces, whole, sems)
    for copy in copies:
        copy.wait()
    rows = 128
    tiles = queries.shape[1] // rows

    def step(n, _):
        for head in range(GROUP):
            r = pl.ds(pl.multiple_of(n * rows, rows), rows)
            scores = lax.dot_general(
                queries[head, r, :], whole[:, :HEAD_DIM], (((1,), (1,)), ((), ())),
                preferred_element_type=jnp.float32,
            )
            scores = scores + mask[r, :]
            top = jnp.max(scores, axis=-1, keepdims=True)
            exponentials = jnp.exp2((scores - top) * SCORE)
            total = jnp.sum(exponentials, axis=-1, keepdims=True)
            summed = jnp.dot(
                exponentials.astype(jnp.bfloat16), whole[:, HEAD_DIM:],
                preferred_element_type=jnp.float32,
            )
            context[r, head * HEAD_DIM : (head + 1) * HEAD_DIM] = (summed / total).astype(jnp.bfloat16)
        return 0

    lax.fori_loop(0, tiles, step, 0)


def attend(ids, queries, mask, pieces):
    tokens = queries.shape[1]
    keys = mask.shape[1]
    any_space = pl.BlockSpec(memory_space=pl.ANY)
    vmem = pl.BlockSpec(memory_space=VMEM)
    return pl.pallas_call(
        attend_kernel,
        out_shape=jax.ShapeDtypeStruct((tokens, QH), jnp.bfloat16),
        in_specs=[pl.BlockSpec(memory_space=SMEM), vmem, vmem] + [any_space] * 16,
        out_specs=vmem,
        scratch_shapes=[
            pltpu.VMEM((keys, 2 * HEAD_DIM), jnp.bfloat16),
            pltpu.SemaphoreType.DMA((16,)),
        ],
        compiler_params=pltpu.CompilerParams(vmem_limit_bytes=24 * 1024 * 1024),
        cost_estimate=pl.CostEstimate(
            flops=4 * tokens * keys * QH, bytes_accessed=8 * 1024 * 1024, transcendentals=tokens * keys * GROUP
        ),
    )(ids, queries, mask, *pieces)


def finish_kernel(ids, own, other, residual, *rest):
    pieces, out, (whole, context, sems) = rest[:16], rest[16], rest[17:]
    copies = start_copies(ids, pieces, whole, sems)
    core = ids[16]
    context[:, pl.ds(pl.multiple_of(core * QH, 128), QH)] = own[...]
    context[:, pl.ds(pl.multiple_of((1 - core) * QH, 128), QH)] = other[...]
    for copy in copies:
        copy.wait()
    for n in range(0, HALF, 256):
        y = jnp.dot(context[...], whole[:, n : n + 256], preferred_element_type=jnp.float32)
        out[:, n : n + 256] = (residual[:, n : n + 256].astype(jnp.float32) + y).astype(jnp.bfloat16)


def finish(ids, own, other, residual, pieces):
    tokens = own.shape[0]
    any_space = pl.BlockSpec(memory_space=pl.ANY)
    vmem = pl.BlockSpec(memory_space=VMEM)
    return pl.pallas_call(
        finish_kernel,
        out_shape=jax.ShapeDtypeStruct((tokens, HALF), jnp.bfloat16),
        in_specs=[pl.BlockSpec(memory_space=SMEM)] + [vmem] * 3 + [any_space] * 16,
        out_specs=vmem,
        scratch_shapes=[
            pltpu.VMEM((2 * QH, HALF), jnp.bfloat16),
            pltpu.VMEM((tokens, 2 * QH), jnp.bfloat16),
            pltpu.SemaphoreType.DMA((16,)),
        ],
        compiler_params=pltpu.CompilerParams(vmem_limit_bytes=24 * 1024 * 1024),
        cost_estimate=pl.CostEstimate(
            flops=4 * tokens * QH * HALF, bytes_accessed=4 * QH * HALF, transcendentals=0
        ),
    )(ids, own, other, residual, *pieces)


def per_device(
    activations, incoming, column_ids, positions, norm_gain, w_query, w_key, w_value, w_out,
    b_query, b_key, b_value,
):
    section = lax.axis_index("section")
    sections = lax.axis_size("section")
    seq = lax.axis_index("seq")
    core = seq % NC
    x = seq // NC % NX
    z = seq // (NC * NX)
    chip = seq // NC
    rows = activations.shape[1]
    tokens = NC * rows
    length = column_ids.shape[1]
    flip = 1 - core

    def cut(value, which, width):
        return lax.dynamic_slice_in_dim(value, which * width, width, value.ndim - 1)

    def columns_of(which):
        return jnp.concatenate(
            [cut(w_query[0], which, QH), cut(w_key[0], which, HEAD_DIM), cut(w_value[0], which, HEAD_DIM)], axis=1
        )

    weight_pieces = spread(columns_of(core), send(columns_of(flip), CORE))
    out_pieces = spread(cut(w_out[0], core, HALF), send(cut(w_out[0], flip, HALF), CORE))
    weight_ids = jnp.concatenate([piece_ids(z, x, core, flip), core[None].astype(jnp.int32)])
    token_ids = piece_ids(z, x, 0, 1)
    bias = jnp.concatenate(
        [cut(b_query, core, QH), cut(b_key, core, HEAD_DIM), cut(b_value, core, HEAD_DIM)], axis=1
    )

    def both_halves(value):
        there = send(value, CORE)
        whole = jnp.where(
            core == 0,
            jnp.concatenate([value, there], axis=0),
            jnp.concatenate([there, value], axis=0),
        )
        return cut(whole, core, HALF), cut(whole, flip, HALF)

    first_own, first_other = both_halves(activations[0])
    in_own, in_other = both_halves(incoming)

    freqs = THETA ** (-(jnp.arange(HEAD_DIM // 2, dtype=jnp.float32) * 2.0) / HEAD_DIM)

    def tables(micro_row):
        places = lax.dynamic_index_in_dim(positions, micro_row, 0, keepdims=False)
        places = lax.dynamic_slice_in_dim(places, chip * tokens, tokens)
        angles = places.astype(jnp.float32)[:, None] * freqs[None, :]
        cosine, sine = jnp.cos(angles), jnp.sin(angles)
        columns = lax.dynamic_index_in_dim(column_ids, micro_row, 0, keepdims=False)
        query_columns = lax.dynamic_slice_in_dim(columns, chip * tokens, tokens)
        query_index = chip * tokens + jnp.arange(tokens, dtype=jnp.int32)
        key_index = jnp.arange(length, dtype=jnp.int32)
        allowed = (key_index[None, :] <= query_index[:, None]) & (
            (columns[None, :] == query_columns[:, None]) | (columns[None, :] == 0)
        )
        return (
            jnp.concatenate([cosine, cosine], axis=1),
            jnp.concatenate([-sine, sine], axis=1),
            jnp.where(allowed, 0.0, -1e30),
        )

    def layer(own, other, table):
        cosine, sine, mask = table
        queries, kv = project(weight_ids, own, other, norm_gain, bias, cosine, sine, weight_pieces)
        kv_pieces = spread(kv[:rows], kv[rows:])
        context = attend(token_ids, queries, mask, kv_pieces)
        return finish(weight_ids, context, send(context, CORE), own, out_pieces)

    def placed(value):
        mine = lax.dynamic_slice_in_dim(value, core * rows, rows)
        there = send(lax.dynamic_slice_in_dim(value, flip * rows, rows), CORE)
        return jnp.where(
            core == 0,
            jnp.concatenate([mine, there], axis=1),
            jnp.concatenate([there, mine], axis=1),
        )[None]

    table_one = tables(section)
    table_two = tables((section + sections) % (sections + 1))
    first = layer(first_own, first_other, table_one)
    passed = lax.ppermute(first, "section", [(n, n + 1) for n in range(sections - 1)])
    second_own = jnp.where(section == 0, in_own, passed)
    second_other = jnp.where(section == 0, in_other, send(passed, CORE))
    second = layer(second_own, second_other, table_two)
    return (placed(first), placed(second))


def solution(mesh):
    placed = (
        P("section", "seq", None),
        P("seq", None),
        P(),
        P(),
        P("section", None),
        P("section", "seq", None),
        P("section", "seq", None),
        P("section", "seq", None),
        P("section", "seq", None),
        P("section", None),
        P("section", None),
        P("section", None),
    )
    return jax.shard_map(
        per_device,
        mesh=mesh,
        in_specs=placed,
        out_specs=(P("section", "seq", None), P("section", "seq", None)),
        check_vma=False,
    )
```

```python
import functools

import jax
import jax.numpy as jnp
from jax import lax
from jax.experimental import pallas as pl
from jax.experimental.pallas import tpu as pltpu
from jax.sharding import PartitionSpec as P

HEAD_DIM = 128
HEADS = 14
KV_HEADS = 2
GROUP = HEADS // KV_HEADS
D = 3584
HALF = D // 2
QH = GROUP * HEAD_DIM
CAT = QH + 2 * HEAD_DIM
EPSILON = 1e-06
THETA = 1000000.0
NZ, NX, NC = 4, 2, 2
CHIPS = NZ * NX
SCORE = HEAD_DIM ** (-0.5) * 1.4426950408889634
SMALL = 2.0**-60
MIB = 1024 * 1024
LIGHT = pl.CostEstimate(flops=1, bytes_accessed=1, transcendentals=0)
QUARTER = HALF // 2
PARTS = (1, 0)
LOCAL = pl.BlockSpec(memory_space=pltpu.MemorySpace.VMEM)
SCALARS = pl.BlockSpec(memory_space=pltpu.MemorySpace.SMEM)
ANYWHERE = pl.BlockSpec(memory_space=pl.ANY)
FAR_MEMORY = pl.BlockSpec(memory_space=pltpu.MemorySpace.HBM)


def shift(move):
    pairs = []
    for z in range(NZ):
        for x in range(NX):
            for c in range(NC):
                a, b, d = move(z, x, c)
                pairs.append(((z * NX + x) * NC + c, ((a % NZ) * NX + b) * NC + d))
    return pairs


UP = shift(lambda z, x, c: (z + 1, x, c))
DOWN = shift(lambda z, x, c: (z - 1, x, c))
ACROSS = shift(lambda z, x, c: (z, 1 - x, c))
FAR = shift(lambda z, x, c: (z + 2, x, c))
CORE = shift(lambda z, x, c: (z, x, 1 - c))


def send(value, pairs):
    return lax.ppermute(value, "seq", pairs)


def after(value, *others):
    return lax.optimization_barrier((value, *others))[0]


def stage_one(first, second):
    return [send(value, pairs) for pairs in (ACROSS, UP, DOWN) for value in (first, second)]


def stage_two(arrived):
    across_a, across_b, up_a, up_b, down_a, down_b = arrived
    return [
        send(across_a, UP), send(across_a, DOWN), send(up_a, UP),
        send(across_b, UP), send(across_b, DOWN), send(down_b, DOWN),
    ]


def stage_three(arrived):
    return [send(arrived[2], ACROSS), send(arrived[5], ACROSS)]


def stage_rows(z, x, first, second):
    here, across = z * NX + x, z * NX + 1 - x
    up, down, far = (z + 3) % NZ * NX, (z + 1) % NZ * NX, (z + 2) % NZ * NX
    own = [here * NC + first, here * NC + second]
    one = [chip * NC + core for chip in (across, up + x, down + x) for core in (first, second)]
    two = [
        (up + 1 - x) * NC + first, (down + 1 - x) * NC + first, (far + x) * NC + first,
        (up + 1 - x) * NC + second, (down + 1 - x) * NC + second, (far + x) * NC + second,
    ]
    three = [(far + 1 - x) * NC + first, (far + 1 - x) * NC + second]
    return own, one, two, three


def spread_small(own):
    across = send(own, ACROSS)
    up, down, far = send(own, UP), send(own, DOWN), send(own, FAR)
    cross_up, cross_down = send(across, UP), send(across, DOWN)
    cross_far = send(far, ACROSS)
    return [own, up, down, across, far, cross_up, cross_down, cross_far]


def chip_ids(z, x):
    return [
        z * NX + x,
        (z + 3) % NZ * NX + x,
        (z + 1) % NZ * NX + x,
        z * NX + 1 - x,
        (z + 2) % NZ * NX + x,
        (z + 3) % NZ * NX + 1 - x,
        (z + 1) % NZ * NX + 1 - x,
        (z + 2) % NZ * NX + 1 - x,
    ]


def start_copies(ids, pieces, whole, sems):
    rows = pieces[0].shape[0]
    copies = []
    for n, piece in enumerate(pieces):
        at = pl.multiple_of(ids[n] * rows, 16)
        copy = pltpu.make_async_copy(piece, whole.at[pl.ds(at, rows)], sems.at[n])
        copy.start()
        copies.append(copy)
    return copies


def project_finish(y, n, cosine, sine, bias, q_out, kv_out):
    y = y + bias[:, n : n + HEAD_DIM]
    if n < QH + HEAD_DIM:
        y = y * cosine[...] + pltpu.roll(y, HEAD_DIM // 2, 1) * sine[...]
    if n < QH:
        q_out[n // HEAD_DIM] = y.astype(jnp.bfloat16)
    else:
        kv_out[:, n - QH : n - QH + HEAD_DIM] = y.astype(jnp.bfloat16)


def project_kernel(ids, hidden, bias, cosine, sine, *rest):
    pieces, (q_out, kv_out) = rest[:16], rest[16:]
    for n in range(0, CAT, 256):
        wide = min(256, CAT - n)
        y = 0.0
        for m, piece in enumerate(pieces):
            y = y + jnp.dot(hidden[ids[2 + m]], piece[:, n : n + wide], preferred_element_type=jnp.float32)
        for m in range(0, wide, HEAD_DIM):
            project_finish(y[:, m : m + HEAD_DIM], n + m, cosine, sine, bias, q_out, kv_out)


def project(ids, hidden, bias, cosine, sine, pieces):
    tokens = hidden.shape[1]
    return pl.pallas_call(
        project_kernel,
        out_shape=(
            jax.ShapeDtypeStruct((GROUP, tokens, HEAD_DIM), jnp.bfloat16),
            jax.ShapeDtypeStruct((tokens, 2 * HEAD_DIM), jnp.bfloat16),
        ),
        in_specs=[SCALARS] + [LOCAL] * 20,
        out_specs=(LOCAL,) * 2,
        compiler_params=pltpu.CompilerParams(vmem_limit_bytes=20 * MIB),
        cost_estimate=LIGHT,
    )(ids, hidden, bias, cosine, sine, *pieces)


def arrange_kernel(ids, *rest):
    pieces, blocks, sems = rest[:16], rest[17:21], rest[21]
    rows = pieces[0].shape[0]
    count = QUARTER // rows
    for m, piece in enumerate(pieces):
        place = ids[2 + m]
        half, inside = place // (2 * count), place % (2 * count)
        which = (half != ids[0]).astype(jnp.int32) * 2 + inside // count
        at = pl.multiple_of(inside % count * rows, 16)
        for n, block in enumerate(blocks):

            @pl.when(which == n)
            def _(piece=piece, block=block, m=m, at=at):
                pltpu.make_async_copy(piece, block.at[pl.ds(at, rows)], sems.at[m]).start()

    for m, piece in enumerate(pieces):
        pltpu.make_async_copy(piece, blocks[0].at[pl.ds(0, rows)], sems.at[m]).wait()


def arrange(ids, pieces, after):
    return pl.pallas_call(
        arrange_kernel,
        out_shape=(jax.ShapeDtypeStruct((QUARTER, CAT), jnp.bfloat16),) * 4,
        in_specs=[SCALARS] + [ANYWHERE] * 17,
        out_specs=(ANYWHERE,) * 4,
        scratch_shapes=[pltpu.SemaphoreType.DMA((16,))],
        compiler_params=pltpu.CompilerParams(vmem_limit_bytes=4 * MIB),
        cost_estimate=LIGHT,
    )(ids, *pieces, after)


def part_sums(ids, part, passed, entered, gain, weights):
    hidden, squares = [], 0.0
    for n, (a, b) in enumerate(zip(passed, entered)):
        value = jnp.where(ids[1] == 0, b[...], a[...]).astype(jnp.float32)
        at = pl.multiple_of((ids[0] if n == 0 else 1 - ids[0]) * HALF + part * QUARTER, 128)
        squares = squares + jnp.sum(value * value, axis=-1, keepdims=True)
        hidden.append((value * (gain[:, pl.ds(at, QUARTER)] * SMALL)).astype(jnp.bfloat16))

    def product(n, wide):
        return jnp.dot(hidden[0], weights[0][:, n : n + wide], preferred_element_type=jnp.float32) + jnp.dot(
            hidden[1], weights[1][:, n : n + wide], preferred_element_type=jnp.float32
        )

    return squares, product


def begin_kernel(ids, own, other, in_own, in_other, gain, w_own, w_other, sums, squares):
    total, product = part_sums(ids, PARTS[0], (own, other), (in_own, in_other), gain, (w_own, w_other))
    squares[...] = total
    for n in range(0, CAT, 256):
        wide = min(256, CAT - n)
        sums[:, n : n + wide] = product(n, wide)


def begin(ids, parts, gain, weights):
    tokens = parts[0].shape[0]
    return pl.pallas_call(
        begin_kernel,
        out_shape=(
            jax.ShapeDtypeStruct((tokens, CAT), jnp.float32),
            jax.ShapeDtypeStruct((tokens, 1), jnp.float32),
        ),
        in_specs=[SCALARS] + [LOCAL] * 7,
        out_specs=(LOCAL,) * 2,
        compiler_params=pltpu.CompilerParams(vmem_limit_bytes=20 * MIB),
        cost_estimate=LIGHT,
    )(ids, *parts, gain, *weights)


def complete_kernel(ids, own, other, in_own, in_other, gain, w_own, w_other, sums, squares, bias, cosine, sine, q_out, kv_out):
    total, product = part_sums(ids, PARTS[1], (own, other), (in_own, in_other), gain, (w_own, w_other))
    inverse = lax.rsqrt((total + squares[...]) * (1.0 / D) + EPSILON) * (1.0 / SMALL)
    for n in range(0, CAT, 256):
        wide = min(256, CAT - n)
        y = (sums[:, n : n + wide] + product(n, wide)) * inverse
        for m in range(0, wide, HEAD_DIM):
            project_finish(y[:, m : m + HEAD_DIM], n + m, cosine, sine, bias, q_out, kv_out)


def complete(ids, parts, gain, weights, sums, squares, bias, cosine, sine):
    tokens = parts[0].shape[0]
    return pl.pallas_call(
        complete_kernel,
        out_shape=(
            jax.ShapeDtypeStruct((GROUP, tokens, HEAD_DIM), jnp.bfloat16),
            jax.ShapeDtypeStruct((tokens, 2 * HEAD_DIM), jnp.bfloat16),
        ),
        in_specs=[SCALARS] + [LOCAL] * 12,
        out_specs=(LOCAL,) * 2,
        compiler_params=pltpu.CompilerParams(vmem_limit_bytes=20 * MIB),
        cost_estimate=LIGHT,
    )(ids, *parts, gain, *weights, sums, squares, bias, cosine, sine)


def attend_kernel(ids, queries, mask, *rest):
    pieces, context, (whole, sems) = rest[:CHIPS], rest[CHIPS], rest[CHIPS + 1 :]
    copies = start_copies(ids, pieces, whole, sems)
    for copy in copies:
        copy.wait()

    def step(head, _):
        scores = lax.dot_general(
            queries[head], whole[:, :HEAD_DIM], (((1,), (1,)), ((), ())),
            preferred_element_type=jnp.float32,
        )
        scores = scores + mask[...]
        top = jnp.max(scores, axis=-1, keepdims=True)
        exponentials = jnp.exp2((scores - top) * SCORE)
        total = jnp.sum(exponentials, axis=-1, keepdims=True)
        summed = jnp.dot(
            exponentials.astype(jnp.bfloat16), whole[:, HEAD_DIM:], preferred_element_type=jnp.float32
        )
        at = pl.ds(pl.multiple_of(head * HEAD_DIM, HEAD_DIM), HEAD_DIM)
        context[:, at] = (summed / total).astype(jnp.bfloat16)
        return 0

    lax.fori_loop(0, GROUP, step, 0)


def attend(ids, queries, mask, pieces):
    tokens = queries.shape[1]
    keys = mask.shape[1]
    return pl.pallas_call(
        attend_kernel,
        out_shape=jax.ShapeDtypeStruct((tokens, QH), jnp.bfloat16),
        in_specs=[SCALARS, LOCAL, LOCAL] + [FAR_MEMORY] * CHIPS,
        out_specs=LOCAL,
        scratch_shapes=[
            pltpu.VMEM((keys, 2 * HEAD_DIM), jnp.bfloat16),
            pltpu.SemaphoreType.DMA((CHIPS,)),
        ],
        compiler_params=pltpu.CompilerParams(vmem_limit_bytes=16 * MIB),
        cost_estimate=LIGHT,
    )(ids, queries, mask, *pieces)


def finish_kernel(part, from_entered, ids, own, other, *rest):
    if part > 0:
        rest = rest[1:]
    if from_entered:
        passed, entered, whole, mine, theirs = rest
    else:
        residual, whole, out = rest
    core = ids[0]
    rows = own.shape[0] // NC
    at_own = pl.ds(pl.multiple_of(core * QH, 128), QH)
    at_other = pl.ds(pl.multiple_of((1 - core) * QH, 128), QH)
    wide = QUARTER // 2
    for n in range(0, QUARTER, wide):
        c = slice(n, n + wide)
        y = jnp.dot(own[...], whole[at_own, c], preferred_element_type=jnp.float32) + jnp.dot(
            other[...], whole[at_other, c], preferred_element_type=jnp.float32
        )
        if from_entered:
            value = jnp.where(ids[1] == 0, entered[:, c], passed[:, c])
        else:
            value = residual[:, c]
        y = (value.astype(jnp.float32) + y).astype(jnp.bfloat16)
        if from_entered:
            low, high = y[:rows], y[rows:]
            mine[:, c] = jnp.where(core == 0, low, high)
            theirs[:, c] = jnp.where(core == 0, high, low)
        else:
            out[:, c] = y


def finish(ids, part, own, other, residual, whole, after=()):
    tokens = own.shape[0]
    from_entered = len(residual) == 2
    if from_entered:
        shapes = (jax.ShapeDtypeStruct((tokens // NC, QUARTER), jnp.bfloat16),) * 2
    else:
        shapes = jax.ShapeDtypeStruct((tokens, QUARTER), jnp.bfloat16)
    return pl.pallas_call(
        functools.partial(finish_kernel, part, from_entered),
        out_shape=shapes,
        in_specs=[SCALARS] + [LOCAL] * 2 + [ANYWHERE] * len(after) + [LOCAL] * (len(residual) + 1),
        out_specs=(LOCAL,) * 2 if from_entered else LOCAL,
        compiler_params=pltpu.CompilerParams(vmem_limit_bytes=20 * MIB),
        cost_estimate=LIGHT,
    )(ids, own, other, *after, *residual, whole)


def per_device(
    activations, incoming, column_ids, positions, norm_gain, w_query, w_key, w_value, w_out,
    b_query, b_key, b_value,
):
    section = lax.axis_index("section")
    sections = lax.axis_size("section")
    seq = lax.axis_index("seq")
    core = seq % NC
    x = seq // NC % NX
    z = seq // (NC * NX)
    chip = seq // NC
    rows = activations.shape[1]
    tokens = NC * rows
    length = column_ids.shape[1]
    flip = 1 - core

    def cut(value, which, width):
        return lax.dynamic_slice_in_dim(value, which * width, width, value.ndim - 1)

    def columns_of(which):
        return jnp.concatenate(
            [cut(w_query[0], which, QH), cut(w_key[0], which, HEAD_DIM), cut(w_value[0], which, HEAD_DIM)], axis=1
        )

    weights, weights_two = columns_of(core), send(columns_of(flip), CORE)
    rows_of = stage_rows(z, x, core, flip)
    one = stage_one(weights, weights_two)
    two = stage_two(one)
    pieces = [weights, weights_two] + one + two + stage_three(two)
    ids = jnp.stack([core, section] + [row for rows_in in rows_of for row in rows_in]).astype(jnp.int32)
    token_ids = jnp.stack(chip_ids(z, x)).astype(jnp.int32)
    bias = jnp.concatenate(
        [cut(b_query, core, QH), cut(b_key, core, HEAD_DIM), cut(b_value, core, HEAD_DIM)], axis=1
    )

    def both_halves(value):
        there = send(value, CORE)
        whole = jnp.where(
            core == 0,
            jnp.concatenate([value, there], axis=0),
            jnp.concatenate([there, value], axis=0),
        )
        return whole

    first_whole, in_whole = both_halves(activations[0]), both_halves(incoming)
    first_own, in_own, in_other = cut(first_whole, core, HALF), cut(in_whole, core, HALF), cut(in_whole, flip, HALF)
    wide = first_whole.astype(jnp.float32)
    hidden = (
        wide * lax.rsqrt(jnp.mean(wide * wide, axis=-1, keepdims=True) + EPSILON) * norm_gain
    ).astype(jnp.bfloat16)
    hidden = jnp.transpose(hidden.reshape(tokens, CHIPS * NC, D // (CHIPS * NC)), (1, 0, 2))

    full_out = lax.all_gather(w_out[0], "seq", axis=0, tiled=True)

    def out_part(part):
        return lax.dynamic_slice_in_dim(full_out, core * HALF + part * QUARTER, QUARTER, 1)

    freqs = THETA ** (-(jnp.arange(HEAD_DIM // 2, dtype=jnp.float32) * 2.0) / HEAD_DIM)

    def tables(micro_row):
        places = lax.dynamic_index_in_dim(positions, micro_row, 0, keepdims=False)
        places = lax.dynamic_slice_in_dim(places, chip * tokens, tokens)
        angles = places.astype(jnp.float32)[:, None] * freqs[None, :]
        cosine, sine = jnp.cos(angles), jnp.sin(angles)
        columns = lax.dynamic_index_in_dim(column_ids, micro_row, 0, keepdims=False)
        query_columns = lax.dynamic_slice_in_dim(columns, chip * tokens, tokens)
        query_index = chip * tokens + jnp.arange(tokens, dtype=jnp.int32)
        key_index = jnp.arange(length, dtype=jnp.int32)
        allowed = (key_index[None, :] <= query_index[:, None]) & (
            (columns[None, :] == query_columns[:, None]) | (columns[None, :] == 0)
        )
        return (
            jnp.concatenate([cosine, cosine], axis=1),
            jnp.concatenate([-sine, sine], axis=1),
            jnp.where(allowed, 0.0, -1e30),
        )

    def placed(mine, there):
        return jnp.where(
            core == 0,
            jnp.concatenate(mine + there, axis=1),
            jnp.concatenate(there + mine, axis=1),
        )[None]

    table_one = tables(section)
    table_two = tables((section + sections) % (sections + 1))
    hidden, bias, table_one, table_two, in_own, in_other, first_own = lax.optimization_barrier(
        (hidden, bias, table_one, table_two, in_own, in_other, first_own)
    )
    queries, kv = project(ids, hidden, bias, *table_one[:2], pieces)
    queries, out_parts = lax.optimization_barrier((queries, [out_part(0), out_part(1)]))
    context = attend(token_ids, queries, table_one[2], spread_small(kv))
    context_other = send(context, CORE)
    first, passed = [], []
    for part in range(2):
        columns = slice(part * QUARTER, (part + 1) * QUARTER)
        first.append(finish(ids, part, context, context_other, (first_own[:, columns],), out_parts[part], first[:part]))
        passed.append(lax.ppermute(first[part], "section", [(n, n + 1) for n in range(sections - 1)]))
    blocks = arrange(ids, pieces, first[1])

    def parts(part, *others):
        columns = slice(part * QUARTER, (part + 1) * QUARTER)
        there = send(after(passed[part], *others), CORE)
        return passed[part], there, in_own[:, columns], in_other[:, columns]

    early, late = PARTS
    sums, squares = begin(ids, parts(early, *blocks), norm_gain, (blocks[early], blocks[2 + early]))
    queries, kv = complete(
        ids, parts(late, sums), norm_gain, (blocks[late], blocks[2 + late]), sums, squares, bias, *table_two[:2]
    )
    context = attend(token_ids, queries, table_two[2], spread_small(kv))
    context_other = send(context, CORE)
    mine, there = [], []
    for part in range(2):
        residual = (passed[part], in_own[:, part * QUARTER : (part + 1) * QUARTER])
        own, theirs = finish(ids, part, context, context_other, residual, out_parts[part], mine[:part])
        mine.append(own)
        there.append(send(theirs, CORE))
    second = placed(mine, there)
    first = jnp.concatenate(first, axis=1)
    first = placed(
        [lax.dynamic_slice_in_dim(first, core * rows, rows)],
        [send(lax.dynamic_slice_in_dim(first, flip * rows, rows), CORE)],
    )
    return (first, second)


def solution(mesh):
    placed = (
        P("section", "seq", None),
        P("seq", None),
        P(),
        P(),
        P("section", None),
        P("section", "seq", None),
        P("section", "seq", None),
        P("section", "seq", None),
        P("section", "seq", None),
        P("section", None),
        P("section", None),
        P("section", None),
    )
    return jax.shard_map(
        per_device,
        mesh=mesh,
        in_specs=placed,
        out_specs=(P("section", "seq", None), P("section", "seq", None)),
        check_vma=False,
    )
```

```python
import functools

import jax
import jax.numpy as jnp
from jax import lax
from jax.experimental import pallas as pl
from jax.experimental.pallas import tpu as pltpu
from jax.sharding import PartitionSpec as P

HEAD_DIM = 128
HEADS = 14
KV_HEADS = 2
GROUP = HEADS // KV_HEADS
D = 3584
HALF = D // 2
QH = GROUP * HEAD_DIM
CAT = QH + 2 * HEAD_DIM
EPSILON = 1e-06
THETA = 1000000.0
NZ, NX, NC = 4, 2, 2
CHIPS = NZ * NX
SCORE = HEAD_DIM ** (-0.5) * 1.4426950408889634
SMALL = 2.0**-60
MIB = 1024 * 1024
LIGHT = pl.CostEstimate(flops=1, bytes_accessed=1, transcendentals=0)
QUARTER = HALF // 2
PARTS = (1, 0)
LOCAL = pl.BlockSpec(memory_space=pltpu.MemorySpace.VMEM)
SCALARS = pl.BlockSpec(memory_space=pltpu.MemorySpace.SMEM)
ANYWHERE = pl.BlockSpec(memory_space=pl.ANY)
FAR_MEMORY = pl.BlockSpec(memory_space=pltpu.MemorySpace.HBM)


def shift(move):
    pairs = []
    for z in range(NZ):
        for x in range(NX):
            for c in range(NC):
                a, b, d = move(z, x, c)
                pairs.append(((z * NX + x) * NC + c, ((a % NZ) * NX + b) * NC + d))
    return pairs


UP = shift(lambda z, x, c: (z + 1, x, c))
DOWN = shift(lambda z, x, c: (z - 1, x, c))
ACROSS = shift(lambda z, x, c: (z, 1 - x, c))
FAR = shift(lambda z, x, c: (z + 2, x, c))
CORE = shift(lambda z, x, c: (z, x, 1 - c))


def send(value, pairs):
    return lax.ppermute(value, "seq", pairs)


def after(value, *others):
    return lax.optimization_barrier((value, *others))[0]


def stage_one(first, second):
    return [send(value, pairs) for pairs in (ACROSS, UP, DOWN) for value in (first, second)]


def stage_two(arrived):
    across_a, across_b, up_a, up_b, down_a, down_b = arrived
    return [
        send(across_a, UP), send(across_a, DOWN), send(up_a, UP),
        send(across_b, UP), send(across_b, DOWN), send(down_b, DOWN),
    ]


def stage_three(arrived):
    return [send(arrived[2], ACROSS), send(arrived[5], ACROSS)]


def stage_rows(z, x, first, second):
    here, across = z * NX + x, z * NX + 1 - x
    up, down, far = (z + 3) % NZ * NX, (z + 1) % NZ * NX, (z + 2) % NZ * NX
    own = [here * NC + first, here * NC + second]
    one = [chip * NC + core for chip in (across, up + x, down + x) for core in (first, second)]
    two = [
        (up + 1 - x) * NC + first, (down + 1 - x) * NC + first, (far + x) * NC + first,
        (up + 1 - x) * NC + second, (down + 1 - x) * NC + second, (far + x) * NC + second,
    ]
    three = [(far + 1 - x) * NC + first, (far + 1 - x) * NC + second]
    return own, one, two, three


def spread_small(own):
    across = send(own, ACROSS)
    up, down, far = send(own, UP), send(own, DOWN), send(own, FAR)
    cross_up, cross_down = send(across, UP), send(across, DOWN)
    cross_far = send(far, ACROSS)
    return [own, up, down, across, far, cross_up, cross_down, cross_far]


def chip_ids(z, x):
    return [
        z * NX + x,
        (z + 3) % NZ * NX + x,
        (z + 1) % NZ * NX + x,
        z * NX + 1 - x,
        (z + 2) % NZ * NX + x,
        (z + 3) % NZ * NX + 1 - x,
        (z + 1) % NZ * NX + 1 - x,
        (z + 2) % NZ * NX + 1 - x,
    ]


def start_copies(ids, pieces, whole, sems):
    rows = pieces[0].shape[0]
    copies = []
    for n, piece in enumerate(pieces):
        at = pl.multiple_of(ids[n] * rows, 16)
        copy = pltpu.make_async_copy(piece, whole.at[pl.ds(at, rows)], sems.at[n])
        copy.start()
        copies.append(copy)
    return copies


def project_finish(y, n, cosine, sine, bias, q_out, kv_out):
    y = y + bias[:, n : n + HEAD_DIM]
    if n < QH + HEAD_DIM:
        y = y * cosine[...] + pltpu.roll(y, HEAD_DIM // 2, 1) * sine[...]
    if n < QH:
        q_out[n // HEAD_DIM] = y.astype(jnp.bfloat16)
    else:
        kv_out[:, n - QH : n - QH + HEAD_DIM] = y.astype(jnp.bfloat16)


def project_kernel(ids, hidden, bias, cosine, sine, *rest):
    pieces, (q_out, kv_out) = rest[:16], rest[16:]
    for n in range(0, CAT, 256):
        wide = min(256, CAT - n)
        y = 0.0
        for m, piece in enumerate(pieces):
            y = y + jnp.dot(hidden[ids[2 + m]], piece[:, n : n + wide], preferred_element_type=jnp.float32)
        for m in range(0, wide, HEAD_DIM):
            project_finish(y[:, m : m + HEAD_DIM], n + m, cosine, sine, bias, q_out, kv_out)


def project(ids, hidden, bias, cosine, sine, pieces):
    tokens = hidden.shape[1]
    return pl.pallas_call(
        project_kernel,
        out_shape=(
            jax.ShapeDtypeStruct((GROUP, tokens, HEAD_DIM), jnp.bfloat16),
            jax.ShapeDtypeStruct((tokens, 2 * HEAD_DIM), jnp.bfloat16),
        ),
        in_specs=[SCALARS] + [LOCAL] * 20,
        out_specs=(LOCAL,) * 2,
        compiler_params=pltpu.CompilerParams(vmem_limit_bytes=20 * MIB),
        cost_estimate=LIGHT,
    )(ids, hidden, bias, cosine, sine, *pieces)


def arrange_kernel(ids, *rest):
    pieces, blocks, sems = rest[:16], rest[17:21], rest[21]
    rows = pieces[0].shape[0]
    count = QUARTER // rows
    for m, piece in enumerate(pieces):
        place = ids[2 + m]
        half, inside = place // (2 * count), place % (2 * count)
        which = (half != ids[0]).astype(jnp.int32) * 2 + inside // count
        at = pl.multiple_of(inside % count * rows, 16)
        for n, block in enumerate(blocks):

            @pl.when(which == n)
            def _(piece=piece, block=block, m=m, at=at):
                pltpu.make_async_copy(piece, block.at[pl.ds(at, rows)], sems.at[m]).start()

    for m, piece in enumerate(pieces):
        pltpu.make_async_copy(piece, blocks[0].at[pl.ds(0, rows)], sems.at[m]).wait()


def arrange(ids, pieces, after):
    return pl.pallas_call(
        arrange_kernel,
        out_shape=(jax.ShapeDtypeStruct((QUARTER, CAT), jnp.bfloat16),) * 4,
        in_specs=[SCALARS] + [ANYWHERE] * 17,
        out_specs=(ANYWHERE,) * 4,
        scratch_shapes=[pltpu.SemaphoreType.DMA((16,))],
        compiler_params=pltpu.CompilerParams(vmem_limit_bytes=4 * MIB),
        cost_estimate=LIGHT,
    )(ids, *pieces, after)


def part_sums(ids, part, passed, entered, gain, weights):
    hidden, squares = [], 0.0
    for n, (a, b) in enumerate(zip(passed, entered)):
        value = jnp.where(ids[1] == 0, b[...], a[...]).astype(jnp.float32)
        at = pl.multiple_of((ids[0] if n == 0 else 1 - ids[0]) * HALF + part * QUARTER, 128)
        squares = squares + jnp.sum(value * value, axis=-1, keepdims=True)
        hidden.append((value * (gain[:, pl.ds(at, QUARTER)] * SMALL)).astype(jnp.bfloat16))

    def product(n, wide):
        return jnp.dot(hidden[0], weights[0][:, n : n + wide], preferred_element_type=jnp.float32) + jnp.dot(
            hidden[1], weights[1][:, n : n + wide], preferred_element_type=jnp.float32
        )

    return squares, product


def begin_kernel(ids, own, other, in_own, in_other, gain, w_own, w_other, sums, squares):
    total, product = part_sums(ids, PARTS[0], (own, other), (in_own, in_other), gain, (w_own, w_other))
    squares[...] = total
    for n in range(0, CAT, 256):
        wide = min(256, CAT - n)
        sums[:, n : n + wide] = product(n, wide)


def begin(ids, parts, gain, weights):
    tokens = parts[0].shape[0]
    return pl.pallas_call(
        begin_kernel,
        out_shape=(
            jax.ShapeDtypeStruct((tokens, CAT), jnp.float32),
            jax.ShapeDtypeStruct((tokens, 1), jnp.float32),
        ),
        in_specs=[SCALARS] + [LOCAL] * 7,
        out_specs=(LOCAL,) * 2,
        compiler_params=pltpu.CompilerParams(vmem_limit_bytes=20 * MIB),
        cost_estimate=LIGHT,
    )(ids, *parts, gain, *weights)


def complete_kernel(ids, own, other, in_own, in_other, gain, w_own, w_other, sums, squares, bias, cosine, sine, q_out, kv_out):
    total, product = part_sums(ids, PARTS[1], (own, other), (in_own, in_other), gain, (w_own, w_other))
    inverse = lax.rsqrt((total + squares[...]) * (1.0 / D) + EPSILON) * (1.0 / SMALL)
    for n in range(0, CAT, 256):
        wide = min(256, CAT - n)
        y = (sums[:, n : n + wide] + product(n, wide)) * inverse
        for m in range(0, wide, HEAD_DIM):
            project_finish(y[:, m : m + HEAD_DIM], n + m, cosine, sine, bias, q_out, kv_out)


def complete(ids, parts, gain, weights, sums, squares, bias, cosine, sine):
    tokens = parts[0].shape[0]
    return pl.pallas_call(
        complete_kernel,
        out_shape=(
            jax.ShapeDtypeStruct((GROUP, tokens, HEAD_DIM), jnp.bfloat16),
            jax.ShapeDtypeStruct((tokens, 2 * HEAD_DIM), jnp.bfloat16),
        ),
        in_specs=[SCALARS] + [LOCAL] * 12,
        out_specs=(LOCAL,) * 2,
        compiler_params=pltpu.CompilerParams(vmem_limit_bytes=20 * MIB),
        cost_estimate=LIGHT,
    )(ids, *parts, gain, *weights, sums, squares, bias, cosine, sine)


def attend_kernel(ids, queries, mask, *rest):
    pieces, context, whole = rest[:CHIPS], rest[CHIPS], rest[CHIPS + 1]
    for n, piece in enumerate(pieces):
        rows = piece.shape[0]
        whole[pl.ds(pl.multiple_of(ids[n] * rows, rows), rows), :] = piece[...]
    for head in range(GROUP):
        scores = lax.dot_general(
            queries[head], whole[:, :HEAD_DIM], (((1,), (1,)), ((), ())),
            preferred_element_type=jnp.float32,
        )
        scores = scores + mask[...]
        top = jnp.max(scores, axis=-1, keepdims=True)
        exponentials = jnp.exp2((scores - top) * SCORE)
        total = jnp.sum(exponentials, axis=-1, keepdims=True)
        summed = jnp.dot(
            exponentials.astype(jnp.bfloat16), whole[:, HEAD_DIM:], preferred_element_type=jnp.float32
        )
        context[:, head * HEAD_DIM : (head + 1) * HEAD_DIM] = (summed / total).astype(jnp.bfloat16)


def attend(ids, queries, mask, pieces):
    tokens = queries.shape[1]
    keys = mask.shape[1]
    return pl.pallas_call(
        attend_kernel,
        out_shape=jax.ShapeDtypeStruct((tokens, QH), jnp.bfloat16),
        in_specs=[SCALARS] + [LOCAL] * (2 + CHIPS),
        out_specs=LOCAL,
        scratch_shapes=[pltpu.VMEM((keys, 2 * HEAD_DIM), jnp.bfloat16)],
        compiler_params=pltpu.CompilerParams(vmem_limit_bytes=16 * MIB),
        cost_estimate=LIGHT,
    )(ids, queries, mask, *pieces)


def finish_kernel(part, from_entered, ids, own, other, *rest):
    if part > 0:
        rest = rest[1:]
    if from_entered:
        passed, entered, whole, mine, theirs = rest
    else:
        residual, whole, out = rest
    core = ids[0]
    rows = own.shape[0] // NC
    at_own = pl.ds(pl.multiple_of(core * QH, 128), QH)
    at_other = pl.ds(pl.multiple_of((1 - core) * QH, 128), QH)
    wide = QUARTER // 2
    for n in range(0, QUARTER, wide):
        c = slice(n, n + wide)
        y = jnp.dot(own[...], whole[at_own, c], preferred_element_type=jnp.float32) + jnp.dot(
            other[...], whole[at_other, c], preferred_element_type=jnp.float32
        )
        if from_entered:
            value = jnp.where(ids[1] == 0, entered[:, c], passed[:, c])
        else:
            value = residual[:, c]
        y = (value.astype(jnp.float32) + y).astype(jnp.bfloat16)
        if from_entered:
            low, high = y[:rows], y[rows:]
            mine[:, c] = jnp.where(core == 0, low, high)
            theirs[:, c] = jnp.where(core == 0, high, low)
        else:
            out[:, c] = y


def finish(ids, part, own, other, residual, whole, after=()):
    tokens = own.shape[0]
    from_entered = len(residual) == 2
    if from_entered:
        shapes = (jax.ShapeDtypeStruct((tokens // NC, QUARTER), jnp.bfloat16),) * 2
    else:
        shapes = jax.ShapeDtypeStruct((tokens, QUARTER), jnp.bfloat16)
    return pl.pallas_call(
        functools.partial(finish_kernel, part, from_entered),
        out_shape=shapes,
        in_specs=[SCALARS] + [LOCAL] * 2 + [ANYWHERE] * len(after) + [LOCAL] * (len(residual) + 1),
        out_specs=(LOCAL,) * 2 if from_entered else LOCAL,
        compiler_params=pltpu.CompilerParams(vmem_limit_bytes=20 * MIB),
        cost_estimate=LIGHT,
    )(ids, own, other, *after, *residual, whole)


def per_device(
    activations, incoming, column_ids, positions, norm_gain, w_query, w_key, w_value, w_out,
    b_query, b_key, b_value,
):
    section = lax.axis_index("section")
    sections = lax.axis_size("section")
    seq = lax.axis_index("seq")
    core = seq % NC
    x = seq // NC % NX
    z = seq // (NC * NX)
    chip = seq // NC
    rows = activations.shape[1]
    tokens = NC * rows
    length = column_ids.shape[1]
    flip = 1 - core

    def cut(value, which, width):
        return lax.dynamic_slice_in_dim(value, which * width, width, value.ndim - 1)

    def columns_of(which):
        return jnp.concatenate(
            [cut(w_query[0], which, QH), cut(w_key[0], which, HEAD_DIM), cut(w_value[0], which, HEAD_DIM)], axis=1
        )

    weights, weights_two = columns_of(core), send(columns_of(flip), CORE)
    rows_of = stage_rows(z, x, core, flip)
    one = stage_one(weights, weights_two)
    two = stage_two(one)
    pieces = [weights, weights_two] + one + two + stage_three(two)
    ids = jnp.stack([core, section] + [row for rows_in in rows_of for row in rows_in]).astype(jnp.int32)
    token_ids = jnp.stack(chip_ids(z, x)).astype(jnp.int32)
    bias = jnp.concatenate(
        [cut(b_query, core, QH), cut(b_key, core, HEAD_DIM), cut(b_value, core, HEAD_DIM)], axis=1
    )

    def both_halves(value):
        there = send(value, CORE)
        whole = jnp.where(
            core == 0,
            jnp.concatenate([value, there], axis=0),
            jnp.concatenate([there, value], axis=0),
        )
        return whole

    first_whole, in_whole = both_halves(activations[0]), both_halves(incoming)
    first_own, in_own, in_other = cut(first_whole, core, HALF), cut(in_whole, core, HALF), cut(in_whole, flip, HALF)
    wide = first_whole.astype(jnp.float32)
    hidden = (
        wide * lax.rsqrt(jnp.mean(wide * wide, axis=-1, keepdims=True) + EPSILON) * norm_gain
    ).astype(jnp.bfloat16)
    hidden = jnp.transpose(hidden.reshape(tokens, CHIPS * NC, D // (CHIPS * NC)), (1, 0, 2))

    full_out = lax.all_gather(w_out[0], "seq", axis=0, tiled=True)

    def out_part(part):
        return lax.dynamic_slice_in_dim(full_out, core * HALF + part * QUARTER, QUARTER, 1)

    freqs = THETA ** (-(jnp.arange(HEAD_DIM // 2, dtype=jnp.float32) * 2.0) / HEAD_DIM)

    def tables(micro_row):
        places = lax.dynamic_index_in_dim(positions, micro_row, 0, keepdims=False)
        places = lax.dynamic_slice_in_dim(places, chip * tokens, tokens)
        angles = places.astype(jnp.float32)[:, None] * freqs[None, :]
        cosine, sine = jnp.cos(angles), jnp.sin(angles)
        columns = lax.dynamic_index_in_dim(column_ids, micro_row, 0, keepdims=False)
        query_columns = lax.dynamic_slice_in_dim(columns, chip * tokens, tokens)
        query_index = chip * tokens + jnp.arange(tokens, dtype=jnp.int32)
        key_index = jnp.arange(length, dtype=jnp.int32)
        allowed = (key_index[None, :] <= query_index[:, None]) & (
            (columns[None, :] == query_columns[:, None]) | (columns[None, :] == 0)
        )
        return (
            jnp.concatenate([cosine, cosine], axis=1),
            jnp.concatenate([-sine, sine], axis=1),
            jnp.where(allowed, 0.0, -1e30),
        )

    def placed(mine, there):
        return jnp.where(
            core == 0,
            jnp.concatenate(mine + there, axis=1),
            jnp.concatenate(there + mine, axis=1),
        )[None]

    table_one = tables(section)
    table_two = tables((section + sections) % (sections + 1))
    hidden, bias, table_one, table_two, in_own, in_other, first_own = lax.optimization_barrier(
        (hidden, bias, table_one, table_two, in_own, in_other, first_own)
    )
    queries, kv = project(ids, hidden, bias, *table_one[:2], pieces)
    queries, out_parts = lax.optimization_barrier((queries, [out_part(0), out_part(1)]))
    context = attend(token_ids, queries, table_one[2], spread_small(kv))
    context_other = send(context, CORE)
    first, passed = [], []
    for part in range(2):
        columns = slice(part * QUARTER, (part + 1) * QUARTER)
        first.append(finish(ids, part, context, context_other, (first_own[:, columns],), out_parts[part], first[:part]))
        passed.append(lax.ppermute(first[part], "section", [(n, n + 1) for n in range(sections - 1)]))
    blocks = arrange(ids, pieces, first[1])

    def parts(part, *others):
        columns = slice(part * QUARTER, (part + 1) * QUARTER)
        there = send(after(passed[part], *others), CORE)
        return passed[part], there, in_own[:, columns], in_other[:, columns]

    early, late = PARTS
    sums, squares = begin(ids, parts(early, *blocks), norm_gain, (blocks[early], blocks[2 + early]))
    queries, kv = complete(
        ids, parts(late, sums), norm_gain, (blocks[late], blocks[2 + late]), sums, squares, bias, *table_two[:2]
    )
    context = attend(token_ids, queries, table_two[2], spread_small(kv))
    context_other = send(context, CORE)
    mine, there = [], []
    for part in range(2):
        residual = (passed[part], in_own[:, part * QUARTER : (part + 1) * QUARTER])
        own, theirs = finish(ids, part, context, context_other, residual, out_parts[part], mine[:part])
        mine.append(own)
        there.append(send(theirs, CORE))
    second = placed(mine, there)
    first = jnp.concatenate(first, axis=1)
    first = placed(
        [lax.dynamic_slice_in_dim(first, core * rows, rows)],
        [send(lax.dynamic_slice_in_dim(first, flip * rows, rows), CORE)],
    )
    return (first, second)


def solution(mesh):
    placed = (
        P("section", "seq", None),
        P("seq", None),
        P(),
        P(),
        P("section", None),
        P("section", "seq", None),
        P("section", "seq", None),
        P("section", "seq", None),
        P("section", "seq", None),
        P("section", None),
        P("section", None),
        P("section", None),
    )
    return jax.shard_map(
        per_device,
        mesh=mesh,
        in_specs=placed,
        out_specs=(P("section", "seq", None), P("section", "seq", None)),
        check_vma=False,
    )
```

```python
import functools

import jax
import jax.numpy as jnp
from jax import lax
from jax.experimental import pallas as pl
from jax.experimental.pallas import tpu as pltpu
from jax.sharding import PartitionSpec as P

HEAD_DIM = 128
HEADS = 14
KV_HEADS = 2
GROUP = HEADS // KV_HEADS
D = 3584
HALF = D // 2
QH = GROUP * HEAD_DIM
CAT = QH + 2 * HEAD_DIM
EPSILON = 1e-06
THETA = 1000000.0
NZ, NX, NC = 4, 2, 2
CHIPS = NZ * NX
SCORE = HEAD_DIM ** (-0.5) * 1.4426950408889634
SMALL = 2.0**-60
MIB = 1024 * 1024
LIGHT = pl.CostEstimate(flops=1, bytes_accessed=1, transcendentals=0)
QUARTER = HALF // 2
PARTS = (1, 0)
LOCAL = pl.BlockSpec(memory_space=pltpu.MemorySpace.VMEM)
SCALARS = pl.BlockSpec(memory_space=pltpu.MemorySpace.SMEM)
ANYWHERE = pl.BlockSpec(memory_space=pl.ANY)
FAR_MEMORY = pl.BlockSpec(memory_space=pltpu.MemorySpace.HBM)


def shift(move):
    pairs = []
    for z in range(NZ):
        for x in range(NX):
            for c in range(NC):
                a, b, d = move(z, x, c)
                pairs.append(((z * NX + x) * NC + c, ((a % NZ) * NX + b) * NC + d))
    return pairs


UP = shift(lambda z, x, c: (z + 1, x, c))
DOWN = shift(lambda z, x, c: (z - 1, x, c))
ACROSS = shift(lambda z, x, c: (z, 1 - x, c))
FAR = shift(lambda z, x, c: (z + 2, x, c))
CORE = shift(lambda z, x, c: (z, x, 1 - c))


def send(value, pairs):
    return lax.ppermute(value, "seq", pairs)


def after(value, *others):
    return lax.optimization_barrier((value, *others))[0]


def stage_one(first, second):
    return [send(value, pairs) for pairs in (ACROSS, UP, DOWN) for value in (first, second)]


def stage_two(arrived):
    across_a, across_b, up_a, up_b, down_a, down_b = arrived
    return [
        send(across_a, UP), send(across_a, DOWN), send(up_a, UP),
        send(across_b, UP), send(across_b, DOWN), send(down_b, DOWN),
    ]


def stage_three(arrived):
    return [send(arrived[2], ACROSS), send(arrived[5], ACROSS)]


def stage_rows(z, x, first, second):
    here, across = z * NX + x, z * NX + 1 - x
    up, down, far = (z + 3) % NZ * NX, (z + 1) % NZ * NX, (z + 2) % NZ * NX
    own = [here * NC + first, here * NC + second]
    one = [chip * NC + core for chip in (across, up + x, down + x) for core in (first, second)]
    two = [
        (up + 1 - x) * NC + first, (down + 1 - x) * NC + first, (far + x) * NC + first,
        (up + 1 - x) * NC + second, (down + 1 - x) * NC + second, (far + x) * NC + second,
    ]
    three = [(far + 1 - x) * NC + first, (far + 1 - x) * NC + second]
    return own, one, two, three


def spread_small(own):
    across = send(own, ACROSS)
    up, down, far = send(own, UP), send(own, DOWN), send(own, FAR)
    cross_up, cross_down = send(across, UP), send(across, DOWN)
    cross_far = send(far, ACROSS)
    return [own, up, down, across, far, cross_up, cross_down, cross_far]


def chip_ids(z, x):
    return [
        z * NX + x,
        (z + 3) % NZ * NX + x,
        (z + 1) % NZ * NX + x,
        z * NX + 1 - x,
        (z + 2) % NZ * NX + x,
        (z + 3) % NZ * NX + 1 - x,
        (z + 1) % NZ * NX + 1 - x,
        (z + 2) % NZ * NX + 1 - x,
    ]


def start_copies(ids, pieces, whole, sems):
    rows = pieces[0].shape[0]
    copies = []
    for n, piece in enumerate(pieces):
        at = pl.multiple_of(ids[n] * rows, 16)
        copy = pltpu.make_async_copy(piece, whole.at[pl.ds(at, rows)], sems.at[n])
        copy.start()
        copies.append(copy)
    return copies


def project_finish(y, n, cosine, sine, bias, q_out, kv_out):
    y = y + bias[:, n : n + HEAD_DIM]
    if n < QH + HEAD_DIM:
        y = y * cosine[...] + pltpu.roll(y, HEAD_DIM // 2, 1) * sine[...]
    if n < QH:
        q_out[n // HEAD_DIM] = y.astype(jnp.bfloat16)
    else:
        kv_out[:, n - QH : n - QH + HEAD_DIM] = y.astype(jnp.bfloat16)


def prepare_kernel(ids, mine, there, gain, hidden, own_first, own_last):
    count, rows = mine.shape[0], 64
    deep = hidden.shape[2]
    for source, place in ((mine, ids[0]), (there, 1 - ids[0])):
        for n in range(0, count, rows):
            r = pl.ds(pl.multiple_of(place * count + n, rows), rows)
            wide = source[n : n + rows, :].astype(jnp.float32)
            inverse = lax.rsqrt(jnp.mean(wide * wide, axis=-1, keepdims=True) + EPSILON)
            value = (wide * inverse * gain[...]).astype(jnp.bfloat16)
            for m in range(hidden.shape[0]):
                hidden[m, r, :] = value[:, m * deep : (m + 1) * deep]
            at = pl.multiple_of(ids[0] * HALF, 128)
            own_first[r, :] = source[n : n + rows, pl.ds(at, QUARTER)]
            own_last[r, :] = source[n : n + rows, pl.ds(at + QUARTER, QUARTER)]


def prepare(ids, mine, there, gain):
    tokens = NC * mine.shape[0]
    count = CHIPS * NC
    return pl.pallas_call(
        prepare_kernel,
        out_shape=(jax.ShapeDtypeStruct((count, tokens, D // count), jnp.bfloat16),)
        + (jax.ShapeDtypeStruct((tokens, QUARTER), jnp.bfloat16),) * 2,
        in_specs=[SCALARS] + [LOCAL] * 3,
        out_specs=(LOCAL,) * 3,
        compiler_params=pltpu.CompilerParams(vmem_limit_bytes=10 * MIB),
        cost_estimate=LIGHT,
    )(ids, mine, there, gain)


def project_kernel(ids, hidden, bias, cosine, sine, *rest):
    pieces, (q_out, kv_out) = rest[:16], rest[16:]
    for n in range(0, CAT, 256):
        wide = min(256, CAT - n)
        y = 0.0
        for m, piece in enumerate(pieces):
            y = y + jnp.dot(hidden[ids[2 + m]], piece[:, n : n + wide], preferred_element_type=jnp.float32)
        for m in range(0, wide, HEAD_DIM):
            project_finish(y[:, m : m + HEAD_DIM], n + m, cosine, sine, bias, q_out, kv_out)


def project(ids, hidden, bias, cosine, sine, pieces):
    tokens = hidden.shape[1]
    return pl.pallas_call(
        project_kernel,
        out_shape=(
            jax.ShapeDtypeStruct((GROUP, tokens, HEAD_DIM), jnp.bfloat16),
            jax.ShapeDtypeStruct((tokens, 2 * HEAD_DIM), jnp.bfloat16),
        ),
        in_specs=[SCALARS] + [LOCAL] * 20,
        out_specs=(LOCAL,) * 2,
        compiler_params=pltpu.CompilerParams(vmem_limit_bytes=20 * MIB),
        cost_estimate=LIGHT,
    )(ids, hidden, bias, cosine, sine, *pieces)


def arrange_kernel(ids, *rest):
    pieces, blocks, sems = rest[:16], rest[17:21], rest[21]
    rows = pieces[0].shape[0]
    count = QUARTER // rows
    for m, piece in enumerate(pieces):
        place = ids[2 + m]
        half, inside = place // (2 * count), place % (2 * count)
        which = (half != ids[0]).astype(jnp.int32) * 2 + inside // count
        at = pl.multiple_of(inside % count * rows, 16)
        for n, block in enumerate(blocks):

            @pl.when(which == n)
            def _(piece=piece, block=block, m=m, at=at):
                pltpu.make_async_copy(piece, block.at[pl.ds(at, rows)], sems.at[m]).start()

    for m, piece in enumerate(pieces):
        pltpu.make_async_copy(piece, blocks[0].at[pl.ds(0, rows)], sems.at[m]).wait()


def arrange(ids, pieces, after):
    return pl.pallas_call(
        arrange_kernel,
        out_shape=(jax.ShapeDtypeStruct((QUARTER, CAT), jnp.bfloat16),) * 4,
        in_specs=[SCALARS] + [ANYWHERE] * 17,
        out_specs=(ANYWHERE,) * 4,
        scratch_shapes=[pltpu.SemaphoreType.DMA((16,))],
        compiler_params=pltpu.CompilerParams(vmem_limit_bytes=4 * MIB),
        cost_estimate=LIGHT,
    )(ids, *pieces, after)


def part_sums(ids, part, passed, entered, gain, weights):
    hidden, squares = [], 0.0
    for n, (a, b) in enumerate(zip(passed, entered)):
        value = jnp.where(ids[1] == 0, b[...], a[...]).astype(jnp.float32)
        at = pl.multiple_of((ids[0] if n == 0 else 1 - ids[0]) * HALF + part * QUARTER, 128)
        squares = squares + jnp.sum(value * value, axis=-1, keepdims=True)
        hidden.append((value * (gain[:, pl.ds(at, QUARTER)] * SMALL)).astype(jnp.bfloat16))

    def product(n, wide):
        return jnp.dot(hidden[0], weights[0][:, n : n + wide], preferred_element_type=jnp.float32) + jnp.dot(
            hidden[1], weights[1][:, n : n + wide], preferred_element_type=jnp.float32
        )

    return squares, product


def begin_kernel(ids, own, other, in_own, in_other, gain, w_own, w_other, sums, squares):
    total, product = part_sums(ids, PARTS[0], (own, other), (in_own, in_other), gain, (w_own, w_other))
    squares[...] = total
    for n in range(0, CAT, 256):
        wide = min(256, CAT - n)
        sums[:, n : n + wide] = product(n, wide)


def begin(ids, parts, gain, weights):
    tokens = parts[0].shape[0]
    return pl.pallas_call(
        begin_kernel,
        out_shape=(
            jax.ShapeDtypeStruct((tokens, CAT), jnp.float32),
            jax.ShapeDtypeStruct((tokens, 1), jnp.float32),
        ),
        in_specs=[SCALARS] + [LOCAL] * 7,
        out_specs=(LOCAL,) * 2,
        compiler_params=pltpu.CompilerParams(vmem_limit_bytes=20 * MIB),
        cost_estimate=LIGHT,
    )(ids, *parts, gain, *weights)


def complete_kernel(ids, own, other, in_own, in_other, gain, w_own, w_other, sums, squares, bias, cosine, sine, q_out, kv_out):
    total, product = part_sums(ids, PARTS[1], (own, other), (in_own, in_other), gain, (w_own, w_other))
    inverse = lax.rsqrt((total + squares[...]) * (1.0 / D) + EPSILON) * (1.0 / SMALL)
    for n in range(0, CAT, 256):
        wide = min(256, CAT - n)
        y = (sums[:, n : n + wide] + product(n, wide)) * inverse
        for m in range(0, wide, HEAD_DIM):
            project_finish(y[:, m : m + HEAD_DIM], n + m, cosine, sine, bias, q_out, kv_out)


def complete(ids, parts, gain, weights, sums, squares, bias, cosine, sine):
    tokens = parts[0].shape[0]
    return pl.pallas_call(
        complete_kernel,
        out_shape=(
            jax.ShapeDtypeStruct((GROUP, tokens, HEAD_DIM), jnp.bfloat16),
            jax.ShapeDtypeStruct((tokens, 2 * HEAD_DIM), jnp.bfloat16),
        ),
        in_specs=[SCALARS] + [LOCAL] * 12,
        out_specs=(LOCAL,) * 2,
        compiler_params=pltpu.CompilerParams(vmem_limit_bytes=20 * MIB),
        cost_estimate=LIGHT,
    )(ids, *parts, gain, *weights, sums, squares, bias, cosine, sine)


def attend_kernel(ids, queries, mask, *rest):
    pieces, context, whole = rest[:CHIPS], rest[CHIPS], rest[CHIPS + 1]
    for n, piece in enumerate(pieces):
        rows = piece.shape[0]
        whole[pl.ds(pl.multiple_of(ids[n] * rows, rows), rows), :] = piece[...]
    for head in range(GROUP):
        scores = lax.dot_general(
            queries[head], whole[:, :HEAD_DIM], (((1,), (1,)), ((), ())),
            preferred_element_type=jnp.float32,
        )
        scores = scores + mask[...]
        top = jnp.max(scores, axis=-1, keepdims=True)
        exponentials = jnp.exp2((scores - top) * SCORE)
        total = jnp.sum(exponentials, axis=-1, keepdims=True)
        summed = jnp.dot(
            exponentials.astype(jnp.bfloat16), whole[:, HEAD_DIM:], preferred_element_type=jnp.float32
        )
        context[:, head * HEAD_DIM : (head + 1) * HEAD_DIM] = (summed / total).astype(jnp.bfloat16)


def attend(ids, queries, mask, pieces):
    tokens = queries.shape[1]
    keys = mask.shape[1]
    return pl.pallas_call(
        attend_kernel,
        out_shape=jax.ShapeDtypeStruct((tokens, QH), jnp.bfloat16),
        in_specs=[SCALARS] + [LOCAL] * (2 + CHIPS),
        out_specs=LOCAL,
        scratch_shapes=[pltpu.VMEM((keys, 2 * HEAD_DIM), jnp.bfloat16)],
        compiler_params=pltpu.CompilerParams(vmem_limit_bytes=16 * MIB),
        cost_estimate=LIGHT,
    )(ids, queries, mask, *pieces)


def finish_kernel(part, from_entered, ids, own, other, *rest):
    if part > 0:
        rest = rest[1:]
    if from_entered:
        passed, entered, whole, mine, theirs = rest
    else:
        residual, whole, out = rest
    core = ids[0]
    rows = own.shape[0] // NC
    at_own = pl.ds(pl.multiple_of(core * QH, 128), QH)
    at_other = pl.ds(pl.multiple_of((1 - core) * QH, 128), QH)
    wide = QUARTER // 2
    for n in range(0, QUARTER, wide):
        c = slice(n, n + wide)
        y = jnp.dot(own[...], whole[at_own, c], preferred_element_type=jnp.float32) + jnp.dot(
            other[...], whole[at_other, c], preferred_element_type=jnp.float32
        )
        if from_entered:
            value = jnp.where(ids[1] == 0, entered[:, c], passed[:, c])
        else:
            value = residual[:, c]
        y = (value.astype(jnp.float32) + y).astype(jnp.bfloat16)
        if from_entered:
            low, high = y[:rows], y[rows:]
            mine[:, c] = jnp.where(core == 0, low, high)
            theirs[:, c] = jnp.where(core == 0, high, low)
        else:
            out[:, c] = y


def finish(ids, part, own, other, residual, whole, after=()):
    tokens = own.shape[0]
    from_entered = len(residual) == 2
    if from_entered:
        shapes = (jax.ShapeDtypeStruct((tokens // NC, QUARTER), jnp.bfloat16),) * 2
    else:
        shapes = jax.ShapeDtypeStruct((tokens, QUARTER), jnp.bfloat16)
    return pl.pallas_call(
        functools.partial(finish_kernel, part, from_entered),
        out_shape=shapes,
        in_specs=[SCALARS] + [LOCAL] * 2 + [ANYWHERE] * len(after) + [LOCAL] * (len(residual) + 1),
        out_specs=(LOCAL,) * 2 if from_entered else LOCAL,
        compiler_params=pltpu.CompilerParams(vmem_limit_bytes=20 * MIB),
        cost_estimate=LIGHT,
    )(ids, own, other, *after, *residual, whole)


def per_device(
    activations, incoming, column_ids, positions, norm_gain, w_query, w_key, w_value, w_out,
    b_query, b_key, b_value,
):
    section = lax.axis_index("section")
    sections = lax.axis_size("section")
    seq = lax.axis_index("seq")
    core = seq % NC
    x = seq // NC % NX
    z = seq // (NC * NX)
    chip = seq // NC
    rows = activations.shape[1]
    tokens = NC * rows
    length = column_ids.shape[1]
    flip = 1 - core

    def cut(value, which, width):
        return lax.dynamic_slice_in_dim(value, which * width, width, value.ndim - 1)

    def columns_of(which):
        return jnp.concatenate(
            [cut(w_query[0], which, QH), cut(w_key[0], which, HEAD_DIM), cut(w_value[0], which, HEAD_DIM)], axis=1
        )

    weights, weights_two = columns_of(core), send(columns_of(flip), CORE)
    rows_of = stage_rows(z, x, core, flip)
    one = stage_one(weights, weights_two)
    two = stage_two(one)
    pieces = [weights, weights_two] + one + two + stage_three(two)
    ids = jnp.stack([core, section] + [row for rows_in in rows_of for row in rows_in]).astype(jnp.int32)
    token_ids = jnp.stack(chip_ids(z, x)).astype(jnp.int32)
    bias = jnp.concatenate(
        [cut(b_query, core, QH), cut(b_key, core, HEAD_DIM), cut(b_value, core, HEAD_DIM)], axis=1
    )

    def both_halves(value):
        there = send(value, CORE)
        whole = jnp.where(
            core == 0,
            jnp.concatenate([value, there], axis=0),
            jnp.concatenate([there, value], axis=0),
        )
        return whole

    in_whole = both_halves(incoming)
    in_own, in_other = cut(in_whole, core, HALF), cut(in_whole, flip, HALF)
    hidden, *first_own = prepare(ids, activations[0], send(activations[0], CORE), norm_gain)
    full_out = lax.all_gather(w_out[0], "seq", axis=0, tiled=True)

    def out_part(part):
        return lax.dynamic_slice_in_dim(full_out, core * HALF + part * QUARTER, QUARTER, 1)

    freqs = THETA ** (-(jnp.arange(HEAD_DIM // 2, dtype=jnp.float32) * 2.0) / HEAD_DIM)

    def tables(micro_row):
        places = lax.dynamic_index_in_dim(positions, micro_row, 0, keepdims=False)
        places = lax.dynamic_slice_in_dim(places, chip * tokens, tokens)
        angles = places.astype(jnp.float32)[:, None] * freqs[None, :]
        cosine, sine = jnp.cos(angles), jnp.sin(angles)
        columns = lax.dynamic_index_in_dim(column_ids, micro_row, 0, keepdims=False)
        query_columns = lax.dynamic_slice_in_dim(columns, chip * tokens, tokens)
        query_index = chip * tokens + jnp.arange(tokens, dtype=jnp.int32)
        key_index = jnp.arange(length, dtype=jnp.int32)
        allowed = (key_index[None, :] <= query_index[:, None]) & (
            (columns[None, :] == query_columns[:, None]) | (columns[None, :] == 0)
        )
        return (
            jnp.concatenate([cosine, cosine], axis=1),
            jnp.concatenate([-sine, sine], axis=1),
            jnp.where(allowed, 0.0, -1e30),
        )

    def placed(mine, there):
        return jnp.where(
            core == 0,
            jnp.concatenate(mine + there, axis=1),
            jnp.concatenate(there + mine, axis=1),
        )[None]

    table_one = tables(section)
    table_two = tables((section + sections) % (sections + 1))
    hidden, bias, table_one, table_two, in_own, in_other, first_own = lax.optimization_barrier(
        (hidden, bias, table_one, table_two, in_own, in_other, first_own)
    )
    queries, kv = project(ids, hidden, bias, *table_one[:2], pieces)
    queries, out_parts = lax.optimization_barrier((queries, [out_part(0), out_part(1)]))
    context = attend(token_ids, queries, table_one[2], spread_small(kv))
    context_other = send(context, CORE)
    first, passed = [], []
    for part in range(2):
        columns = slice(part * QUARTER, (part + 1) * QUARTER)
        first.append(finish(ids, part, context, context_other, (first_own[part],), out_parts[part], first[:part]))
        passed.append(lax.ppermute(first[part], "section", [(n, n + 1) for n in range(sections - 1)]))
    blocks = arrange(ids, pieces, first[1])

    def parts(part, *others):
        columns = slice(part * QUARTER, (part + 1) * QUARTER)
        there = send(after(passed[part], *others), CORE)
        return passed[part], there, in_own[:, columns], in_other[:, columns]

    early, late = PARTS
    sums, squares = begin(ids, parts(early, *blocks), norm_gain, (blocks[early], blocks[2 + early]))
    queries, kv = complete(
        ids, parts(late, sums), norm_gain, (blocks[late], blocks[2 + late]), sums, squares, bias, *table_two[:2]
    )
    context = attend(token_ids, queries, table_two[2], spread_small(kv))
    context_other = send(context, CORE)
    mine, there = [], []
    for part in range(2):
        residual = (passed[part], in_own[:, part * QUARTER : (part + 1) * QUARTER])
        own, theirs = finish(ids, part, context, context_other, residual, out_parts[part], mine[:part])
        mine.append(own)
        there.append(send(theirs, CORE))
    second = placed(mine, there)
    first = jnp.concatenate(first, axis=1)
    first = placed(
        [lax.dynamic_slice_in_dim(first, core * rows, rows)],
        [send(lax.dynamic_slice_in_dim(first, flip * rows, rows), CORE)],
    )
    return (first, second)


def solution(mesh):
    placed = (
        P("section", "seq", None),
        P("seq", None),
        P(),
        P(),
        P("section", None),
        P("section", "seq", None),
        P("section", "seq", None),
        P("section", "seq", None),
        P("section", "seq", None),
        P("section", None),
        P("section", None),
        P("section", None),
    )
    return jax.shard_map(
        per_device,
        mesh=mesh,
        in_specs=placed,
        out_specs=(P("section", "seq", None), P("section", "seq", None)),
        check_vma=False,
    )
```

```python
import functools

import jax
import jax.numpy as jnp
from jax import lax
from jax.experimental import pallas as pl
from jax.experimental.pallas import tpu as pltpu
from jax.sharding import PartitionSpec as P

HEAD_DIM = 128
HEADS = 14
KV_HEADS = 2
GROUP = HEADS // KV_HEADS
D = 3584
HALF = D // 2
QH = GROUP * HEAD_DIM
CAT = QH + 2 * HEAD_DIM
EPSILON = 1e-06
THETA = 1000000.0
NZ, NX, NC = 4, 2, 2
CHIPS = NZ * NX
SCORE = HEAD_DIM ** (-0.5) * 1.4426950408889634
SMALL = 2.0**-60
MIB = 1024 * 1024
LIGHT = pl.CostEstimate(flops=1, bytes_accessed=1, transcendentals=0)
QUARTER = HALF // 2
PARTS = (1, 0)
LOCAL = pl.BlockSpec(memory_space=pltpu.MemorySpace.VMEM)
SCALARS = pl.BlockSpec(memory_space=pltpu.MemorySpace.SMEM)
ANYWHERE = pl.BlockSpec(memory_space=pl.ANY)
FAR_MEMORY = pl.BlockSpec(memory_space=pltpu.MemorySpace.HBM)


def shift(move):
    pairs = []
    for z in range(NZ):
        for x in range(NX):
            for c in range(NC):
                a, b, d = move(z, x, c)
                pairs.append(((z * NX + x) * NC + c, ((a % NZ) * NX + b) * NC + d))
    return pairs


UP = shift(lambda z, x, c: (z + 1, x, c))
DOWN = shift(lambda z, x, c: (z - 1, x, c))
ACROSS = shift(lambda z, x, c: (z, 1 - x, c))
FAR = shift(lambda z, x, c: (z + 2, x, c))
CORE = shift(lambda z, x, c: (z, x, 1 - c))


def send(value, pairs):
    return lax.ppermute(value, "seq", pairs)


def after(value, *others):
    return lax.optimization_barrier((value, *others))[0]


def stage_one(first, second):
    return [send(value, pairs) for pairs in (ACROSS, UP, DOWN) for value in (first, second)]


def stage_two(arrived):
    across_a, across_b, up_a, up_b, down_a, down_b = arrived
    return [
        send(across_a, UP), send(across_a, DOWN), send(up_a, UP),
        send(across_b, UP), send(across_b, DOWN), send(down_b, DOWN),
    ]


def stage_three(arrived):
    return [send(arrived[2], ACROSS), send(arrived[5], ACROSS)]


def stage_rows(z, x, first, second):
    here, across = z * NX + x, z * NX + 1 - x
    up, down, far = (z + 3) % NZ * NX, (z + 1) % NZ * NX, (z + 2) % NZ * NX
    own = [here * NC + first, here * NC + second]
    one = [chip * NC + core for chip in (across, up + x, down + x) for core in (first, second)]
    two = [
        (up + 1 - x) * NC + first, (down + 1 - x) * NC + first, (far + x) * NC + first,
        (up + 1 - x) * NC + second, (down + 1 - x) * NC + second, (far + x) * NC + second,
    ]
    three = [(far + 1 - x) * NC + first, (far + 1 - x) * NC + second]
    return own, one, two, three


def spread_small(own):
    across = send(own, ACROSS)
    up, down, far = send(own, UP), send(own, DOWN), send(own, FAR)
    cross_up, cross_down = send(across, UP), send(across, DOWN)
    cross_far = send(far, ACROSS)
    return [own, up, down, across, far, cross_up, cross_down, cross_far]


def chip_ids(z, x):
    return [
        z * NX + x,
        (z + 3) % NZ * NX + x,
        (z + 1) % NZ * NX + x,
        z * NX + 1 - x,
        (z + 2) % NZ * NX + x,
        (z + 3) % NZ * NX + 1 - x,
        (z + 1) % NZ * NX + 1 - x,
        (z + 2) % NZ * NX + 1 - x,
    ]


def start_copies(ids, pieces, whole, sems):
    rows = pieces[0].shape[0]
    copies = []
    for n, piece in enumerate(pieces):
        at = pl.multiple_of(ids[n] * rows, 16)
        copy = pltpu.make_async_copy(piece, whole.at[pl.ds(at, rows)], sems.at[n])
        copy.start()
        copies.append(copy)
    return copies


def project_finish(y, n, cosine, sine, bias, q_out, kv_out):
    y = y + bias[:, n : n + HEAD_DIM]
    if n < QH + HEAD_DIM:
        y = y * cosine[...] + pltpu.roll(y, HEAD_DIM // 2, 1) * sine[...]
    if n < QH:
        q_out[n // HEAD_DIM] = y.astype(jnp.bfloat16)
    else:
        kv_out[:, n - QH : n - QH + HEAD_DIM] = y.astype(jnp.bfloat16)


def prepare_kernel(ids, mine, there, gain, hidden, own_first, own_last):
    count, rows = mine.shape[0], 64
    deep = hidden.shape[2]
    for source, place in ((mine, ids[0]), (there, 1 - ids[0])):
        for n in range(0, count, rows):
            r = pl.ds(pl.multiple_of(place * count + n, rows), rows)
            wide = source[n : n + rows, :].astype(jnp.float32)
            inverse = lax.rsqrt(jnp.mean(wide * wide, axis=-1, keepdims=True) + EPSILON)
            value = (wide * inverse * gain[...]).astype(jnp.bfloat16)
            for m in range(hidden.shape[0]):
                hidden[m, r, :] = value[:, m * deep : (m + 1) * deep]
            at = pl.multiple_of(ids[0] * HALF, 128)
            own_first[r, :] = source[n : n + rows, pl.ds(at, QUARTER)]
            own_last[r, :] = source[n : n + rows, pl.ds(at + QUARTER, QUARTER)]


def prepare(ids, mine, there, gain):
    tokens = NC * mine.shape[0]
    count = CHIPS * NC
    return pl.pallas_call(
        prepare_kernel,
        out_shape=(jax.ShapeDtypeStruct((count, tokens, D // count), jnp.bfloat16),)
        + (jax.ShapeDtypeStruct((tokens, QUARTER), jnp.bfloat16),) * 2,
        in_specs=[SCALARS] + [LOCAL] * 3,
        out_specs=(LOCAL,) * 3,
        compiler_params=pltpu.CompilerParams(vmem_limit_bytes=10 * MIB),
        cost_estimate=LIGHT,
    )(ids, mine, there, gain)


def project_kernel(ids, hidden, bias, cosine, sine, *rest):
    pieces, (q_out, kv_out) = rest[:16], rest[16:]
    for n in range(0, CAT, 256):
        wide = min(256, CAT - n)
        y = 0.0
        for m, piece in enumerate(pieces):
            y = y + jnp.dot(hidden[ids[2 + m]], piece[:, n : n + wide], preferred_element_type=jnp.float32)
        for m in range(0, wide, HEAD_DIM):
            project_finish(y[:, m : m + HEAD_DIM], n + m, cosine, sine, bias, q_out, kv_out)


def project(ids, hidden, bias, cosine, sine, pieces):
    tokens = hidden.shape[1]
    return pl.pallas_call(
        project_kernel,
        out_shape=(
            jax.ShapeDtypeStruct((GROUP, tokens, HEAD_DIM), jnp.bfloat16),
            jax.ShapeDtypeStruct((tokens, 2 * HEAD_DIM), jnp.bfloat16),
        ),
        in_specs=[SCALARS] + [LOCAL] * 20,
        out_specs=(LOCAL,) * 2,
        compiler_params=pltpu.CompilerParams(vmem_limit_bytes=20 * MIB),
        cost_estimate=LIGHT,
    )(ids, hidden, bias, cosine, sine, *pieces)


def arrange_kernel(ids, *rest):
    pieces, blocks, sems = rest[:16], rest[17:21], rest[21]
    rows = pieces[0].shape[0]
    count = QUARTER // rows
    for m, piece in enumerate(pieces):
        place = ids[2 + m]
        half, inside = place // (2 * count), place % (2 * count)
        which = (half != ids[0]).astype(jnp.int32) * 2 + inside // count
        at = pl.multiple_of(inside % count * rows, 16)
        for n, block in enumerate(blocks):

            @pl.when(which == n)
            def _(piece=piece, block=block, m=m, at=at):
                pltpu.make_async_copy(piece, block.at[pl.ds(at, rows)], sems.at[m]).start()

    for m, piece in enumerate(pieces):
        pltpu.make_async_copy(piece, blocks[0].at[pl.ds(0, rows)], sems.at[m]).wait()


def arrange(ids, pieces, after):
    return pl.pallas_call(
        arrange_kernel,
        out_shape=(jax.ShapeDtypeStruct((QUARTER, CAT), jnp.bfloat16),) * 4,
        in_specs=[SCALARS] + [ANYWHERE] * 17,
        out_specs=(ANYWHERE,) * 4,
        scratch_shapes=[pltpu.SemaphoreType.DMA((16,))],
        compiler_params=pltpu.CompilerParams(vmem_limit_bytes=4 * MIB),
        cost_estimate=LIGHT,
    )(ids, *pieces, after)


def part_sums(ids, part, passed, entered, gain, weights):
    hidden, squares = [], 0.0
    for n, (a, b) in enumerate(zip(passed, entered)):
        value = jnp.where(ids[1] == 0, b[...], a[...]).astype(jnp.float32)
        at = pl.multiple_of((ids[0] if n == 0 else 1 - ids[0]) * HALF + part * QUARTER, 128)
        squares = squares + jnp.sum(value * value, axis=-1, keepdims=True)
        hidden.append((value * (gain[:, pl.ds(at, QUARTER)] * SMALL)).astype(jnp.bfloat16))

    def product(n, wide):
        return jnp.dot(hidden[0], weights[0][:, n : n + wide], preferred_element_type=jnp.float32) + jnp.dot(
            hidden[1], weights[1][:, n : n + wide], preferred_element_type=jnp.float32
        )

    return squares, product


def begin_kernel(ids, own, other, in_own, in_other, gain, w_own, w_other, sums, squares):
    total, product = part_sums(ids, PARTS[0], (own, other), (in_own, in_other), gain, (w_own, w_other))
    squares[...] = total
    for n in range(0, CAT, 256):
        wide = min(256, CAT - n)
        sums[:, n : n + wide] = product(n, wide)


def begin(ids, parts, gain, weights):
    tokens = parts[0].shape[0]
    return pl.pallas_call(
        begin_kernel,
        out_shape=(
            jax.ShapeDtypeStruct((tokens, CAT), jnp.float32),
            jax.ShapeDtypeStruct((tokens, 1), jnp.float32),
        ),
        in_specs=[SCALARS] + [LOCAL] * 7,
        out_specs=(LOCAL,) * 2,
        compiler_params=pltpu.CompilerParams(vmem_limit_bytes=20 * MIB),
        cost_estimate=LIGHT,
    )(ids, *parts, gain, *weights)


def complete_kernel(ids, own, other, in_own, in_other, gain, w_own, w_other, sums, squares, bias, cosine, sine, q_out, kv_out):
    total, product = part_sums(ids, PARTS[1], (own, other), (in_own, in_other), gain, (w_own, w_other))
    inverse = lax.rsqrt((total + squares[...]) * (1.0 / D) + EPSILON) * (1.0 / SMALL)
    for n in range(0, CAT, 256):
        wide = min(256, CAT - n)
        y = (sums[:, n : n + wide] + product(n, wide)) * inverse
        for m in range(0, wide, HEAD_DIM):
            project_finish(y[:, m : m + HEAD_DIM], n + m, cosine, sine, bias, q_out, kv_out)


def complete(ids, parts, gain, weights, sums, squares, bias, cosine, sine):
    tokens = parts[0].shape[0]
    return pl.pallas_call(
        complete_kernel,
        out_shape=(
            jax.ShapeDtypeStruct((GROUP, tokens, HEAD_DIM), jnp.bfloat16),
            jax.ShapeDtypeStruct((tokens, 2 * HEAD_DIM), jnp.bfloat16),
        ),
        in_specs=[SCALARS] + [LOCAL] * 12,
        out_specs=(LOCAL,) * 2,
        compiler_params=pltpu.CompilerParams(vmem_limit_bytes=20 * MIB),
        cost_estimate=LIGHT,
    )(ids, *parts, gain, *weights, sums, squares, bias, cosine, sine)


def attend_kernel(ids, queries, mask, *rest):
    pieces, context, whole = rest[:CHIPS], rest[CHIPS], rest[CHIPS + 1]
    for n, piece in enumerate(pieces):
        rows = piece.shape[0]
        whole[pl.ds(pl.multiple_of(ids[n] * rows, rows), rows), :] = piece[...]
    for head in range(GROUP):
        scores = lax.dot_general(
            queries[head], whole[:, :HEAD_DIM], (((1,), (1,)), ((), ())),
            preferred_element_type=jnp.float32,
        )
        scores = scores + mask[...]
        top = jnp.max(scores, axis=-1, keepdims=True)
        exponentials = jnp.exp2((scores - top) * SCORE)
        total = jnp.sum(exponentials, axis=-1, keepdims=True)
        summed = jnp.dot(
            exponentials.astype(jnp.bfloat16), whole[:, HEAD_DIM:], preferred_element_type=jnp.float32
        )
        context[:, head * HEAD_DIM : (head + 1) * HEAD_DIM] = (summed / total).astype(jnp.bfloat16)


def attend(ids, queries, mask, pieces):
    tokens = queries.shape[1]
    keys = mask.shape[1]
    return pl.pallas_call(
        attend_kernel,
        out_shape=jax.ShapeDtypeStruct((tokens, QH), jnp.bfloat16),
        in_specs=[SCALARS] + [LOCAL] * (2 + CHIPS),
        out_specs=LOCAL,
        scratch_shapes=[pltpu.VMEM((keys, 2 * HEAD_DIM), jnp.bfloat16)],
        compiler_params=pltpu.CompilerParams(vmem_limit_bytes=16 * MIB),
        cost_estimate=LIGHT,
    )(ids, queries, mask, *pieces)


def finish_kernel(part, from_entered, ids, own, other, *rest):
    if part > 0:
        rest = rest[1:]
    if from_entered:
        passed, entered, whole, mine, theirs = rest
    else:
        residual, whole, out = rest
    core = ids[0]
    rows = own.shape[0] // NC
    at_own = pl.ds(pl.multiple_of(core * QH, 128), QH)
    at_other = pl.ds(pl.multiple_of((1 - core) * QH, 128), QH)
    wide = QUARTER // 2
    for n in range(0, QUARTER, wide):
        c = slice(n, n + wide)
        y = jnp.dot(own[...], whole[at_own, c], preferred_element_type=jnp.float32) + jnp.dot(
            other[...], whole[at_other, c], preferred_element_type=jnp.float32
        )
        if from_entered:
            value = jnp.where(ids[1] == 0, entered[:, c], passed[:, c])
        else:
            value = residual[:, c]
        y = (value.astype(jnp.float32) + y).astype(jnp.bfloat16)
        if from_entered:
            low, high = y[:rows], y[rows:]
            mine[:, c] = jnp.where(core == 0, low, high)
            theirs[:, c] = jnp.where(core == 0, high, low)
        else:
            out[:, c] = y


def finish(ids, part, own, other, residual, whole, after=()):
    tokens = own.shape[0]
    from_entered = len(residual) == 2
    if from_entered:
        shapes = (jax.ShapeDtypeStruct((tokens // NC, QUARTER), jnp.bfloat16),) * 2
    else:
        shapes = jax.ShapeDtypeStruct((tokens, QUARTER), jnp.bfloat16)
    return pl.pallas_call(
        functools.partial(finish_kernel, part, from_entered),
        out_shape=shapes,
        in_specs=[SCALARS] + [LOCAL] * 2 + [ANYWHERE] * len(after) + [LOCAL] * (len(residual) + 1),
        out_specs=(LOCAL,) * 2 if from_entered else LOCAL,
        compiler_params=pltpu.CompilerParams(vmem_limit_bytes=20 * MIB),
        cost_estimate=LIGHT,
    )(ids, own, other, *after, *residual, whole)


def per_device(
    activations, incoming, column_ids, positions, norm_gain, w_query, w_key, w_value, w_out,
    b_query, b_key, b_value,
):
    section = lax.axis_index("section")
    sections = lax.axis_size("section")
    seq = lax.axis_index("seq")
    core = seq % NC
    x = seq // NC % NX
    z = seq // (NC * NX)
    chip = seq // NC
    rows = activations.shape[1]
    tokens = NC * rows
    length = column_ids.shape[1]
    flip = 1 - core

    def cut(value, which, width):
        return lax.dynamic_slice_in_dim(value, which * width, width, value.ndim - 1)

    def columns_of(which):
        return jnp.concatenate(
            [cut(w_query[0], which, QH), cut(w_key[0], which, HEAD_DIM), cut(w_value[0], which, HEAD_DIM)], axis=1
        )

    weights, weights_two = columns_of(core), send(columns_of(flip), CORE)
    rows_of = stage_rows(z, x, core, flip)
    one = stage_one(weights, weights_two)
    two = stage_two(one)
    pieces = [weights, weights_two] + one + two + stage_three(two)
    ids = jnp.stack([core, section] + [row for rows_in in rows_of for row in rows_in]).astype(jnp.int32)
    token_ids = jnp.stack(chip_ids(z, x)).astype(jnp.int32)
    bias = jnp.concatenate(
        [cut(b_query, core, QH), cut(b_key, core, HEAD_DIM), cut(b_value, core, HEAD_DIM)], axis=1
    )

    def both_halves(value):
        there = send(value, CORE)
        whole = jnp.where(
            core == 0,
            jnp.concatenate([value, there], axis=0),
            jnp.concatenate([there, value], axis=0),
        )
        return whole

    in_whole = both_halves(incoming)
    in_own, in_other = cut(in_whole, core, HALF), cut(in_whole, flip, HALF)
    hidden, *first_own = prepare(ids, activations[0], send(activations[0], CORE), norm_gain)
    full_out = lax.all_gather(w_out[0], "seq", axis=0, tiled=True)

    def out_part(part):
        return lax.dynamic_slice_in_dim(full_out, core * HALF + part * QUARTER, QUARTER, 1)

    freqs = THETA ** (-(jnp.arange(HEAD_DIM // 2, dtype=jnp.float32) * 2.0) / HEAD_DIM)

    def tables(micro_row):
        places = lax.dynamic_index_in_dim(positions, micro_row, 0, keepdims=False)
        places = lax.dynamic_slice_in_dim(places, chip * tokens, tokens)
        angles = places.astype(jnp.float32)[:, None] * freqs[None, :]
        cosine, sine = jnp.cos(angles), jnp.sin(angles)
        columns = lax.dynamic_index_in_dim(column_ids, micro_row, 0, keepdims=False)
        query_columns = lax.dynamic_slice_in_dim(columns, chip * tokens, tokens)
        query_index = chip * tokens + jnp.arange(tokens, dtype=jnp.int32)
        key_index = jnp.arange(length, dtype=jnp.int32)
        allowed = (key_index[None, :] <= query_index[:, None]) & (
            (columns[None, :] == query_columns[:, None]) | (columns[None, :] == 0)
        )
        return (
            jnp.concatenate([cosine, cosine], axis=1),
            jnp.concatenate([-sine, sine], axis=1),
            jnp.where(allowed, 0.0, -1e30),
        )

    def placed(mine, there):
        return jnp.where(
            core == 0,
            jnp.concatenate(mine + there, axis=1),
            jnp.concatenate(there + mine, axis=1),
        )[None]

    table_one = tables(section)
    table_two = tables((section + sections) % (sections + 1))
    hidden, bias, table_one, table_two, in_own, in_other, first_own = lax.optimization_barrier(
        (hidden, bias, table_one, table_two, in_own, in_other, first_own)
    )
    queries, kv = project(ids, hidden, bias, *table_one[:2], pieces)
    queries, out_parts = lax.optimization_barrier((queries, [out_part(0), out_part(1)]))
    context = attend(token_ids, queries, table_one[2], spread_small(kv))
    context_other = send(context, CORE)
    first, passed = [], []
    for part in range(2):
        columns = slice(part * QUARTER, (part + 1) * QUARTER)
        first.append(finish(ids, part, context, context_other, (first_own[part],), out_parts[part], first[:part]))
        passed.append(lax.ppermute(first[part], "section", [(n, n + 1) for n in range(sections - 1)]))
    blocks = arrange(ids, pieces, first[1])
    first = jnp.concatenate(first, axis=1)
    first = placed(
        [lax.dynamic_slice_in_dim(first, core * rows, rows)],
        [send(lax.dynamic_slice_in_dim(first, flip * rows, rows), CORE)],
    )

    def parts(part, *others):
        columns = slice(part * QUARTER, (part + 1) * QUARTER)
        there = send(after(passed[part], *others), CORE)
        return passed[part], there, in_own[:, columns], in_other[:, columns]

    early, late = PARTS
    sums, squares = begin(ids, parts(early, *blocks), norm_gain, (blocks[early], blocks[2 + early]))
    queries, kv = complete(
        ids, parts(late, sums, first), norm_gain, (blocks[late], blocks[2 + late]), sums, squares, bias, *table_two[:2]
    )
    context = attend(token_ids, queries, table_two[2], spread_small(kv))
    context_other = send(context, CORE)
    mine, there = [], []
    for part in range(2):
        residual = (passed[part], in_own[:, part * QUARTER : (part + 1) * QUARTER])
        own, theirs = finish(ids, part, context, context_other, residual, out_parts[part], mine[:part])
        mine.append(own)
        there.append(send(theirs, CORE))
    second = placed(mine, there)
    return (first, second)


def solution(mesh):
    placed = (
        P("section", "seq", None),
        P("seq", None),
        P(),
        P(),
        P("section", None),
        P("section", "seq", None),
        P("section", "seq", None),
        P("section", "seq", None),
        P("section", "seq", None),
        P("section", None),
        P("section", None),
        P("section", None),
    )
    return jax.shard_map(
        per_device,
        mesh=mesh,
        in_specs=placed,
        out_specs=(P("section", "seq", None), P("section", "seq", None)),
        check_vma=False,
    )
```
